32 devices in a mesh: row: 4 (over y, core), col: 8 (over z, x).
Axes of the slice: x: 2, y: 2, z: 4, core: 2. Of those that a mesh axis runs over, the one named last changes fastest.
Arguments:
- slab: float32 [16384, 8192], P(('row', 'col')), may hold values from -80 to 80, as said below
- sketch: float32 [8192, 128], replicated, may hold values from -0.0625 to 0.0625
Outputs:
- basis: float32 [16384, 128], P(('row', 'col'))
- projection: float32 [128, 8192], replicated
The draws below stay inside these ranges and needn't reach their ends.
Inputs may be any that keep to these rules, and one draw needn't show every extreme that they name: `slab`: each entry is one hidden-state value.
All inputs are finite; a program needn't handle non-finite values.
Results may differ from the reference program's by a relative error of at most 0.000084.
Values sent between devices are 32-bit elements; how exact they have to be, the bound alone decides.
A program may use at most 128 MiB of HBM per device.

```python
import math
import jax
import jax.numpy as jnp
from jax import lax

D = 8192
K = 128
ROWS = 16384


def draw_slab(key, part):
    key = jax.random.fold_in(key, 11)
    key_noise, key_rows, key_cols = jax.random.split(key, 3)
    col_scale = jnp.exp(jax.random.uniform(key_cols, (1, D), jnp.float32, math.log(0.5), math.log(2.0)))
    noise = jnp.clip(jax.random.normal(key_noise, (ROWS, D), jnp.float32), -6.0, 6.0)
    row_scale = jnp.exp(jax.random.uniform(key_rows, (ROWS, 1), jnp.float32, 0.0, math.log(4.0)))
    return noise * row_scale * col_scale


def gaussian(own_key, extent, deviation, most, dtype=jnp.bfloat16):
    return jnp.clip(deviation * jax.random.normal(own_key, extent, jnp.float32), -most, most).astype(dtype)


def setup_inputs(seed: int = 0) -> dict:
    key_list = jax.random.split(jax.random.key(seed), 3)
    return {
        "slab": draw_slab(jax.random.fold_in(key_list[2], 71), 0),
        "sketch": gaussian(key_list[1], (D, K), D ** -0.5, 0.0625, jnp.float32),
    }


def reference(slab, sketch):
    highest = lax.Precision.HIGHEST
    sampled = jnp.dot(slab.astype(jnp.float32), sketch.astype(jnp.float32), precision=highest, preferred_element_type=jnp.float32)
    gram = jnp.dot(sampled.T, sampled, precision=highest)
    lower = jnp.linalg.cholesky(gram)
    transposed = jax.scipy.linalg.solve_triangular(lower, sampled.T, lower=True)
    basis = transposed.T * math.sqrt(ROWS)
    projection = jnp.dot(transposed, slab, precision=highest)
    return (basis, projection)
```

```python
import functools
import math

import jax
import jax.numpy as jnp
from jax import lax
from jax.experimental import pallas as pl
from jax.experimental.pallas import tpu as pltpu
from jax.sharding import PartitionSpec as P

MESH = pl.DeviceIdType.MESH
BF16 = jnp.bfloat16
F32 = jnp.float32
LANES = 128
TILE = 8
LOAD = 512
WIDE = 256
CHUNKS = 8
CHOL = 16


def split(value):
    high = value.astype(BF16)
    return high, (value - high.astype(F32)).astype(BF16)


def bit_of(axis, bit):
    index = lax.axis_index(axis)
    value = (index // 2**bit) % 2
    return {axis: 2**bit * (1 - 2 * value)}, value


def chunk_order(chunk, rows, cols):
    row_bits = [("row", b) for b in range(1, rows.bit_length() - 1)]
    col_bits = [("col", b) for b in range(cols.bit_length() - 1)]
    inner = 1 if len(col_bits) == 3 else len(col_bits) // 2
    near, far = col_bits[:inner], col_bits[inner:]
    core = [("row", 0)]
    if chunk % 3 == 2:
        return core + near + row_bits + far, core + row_bits + near + far
    return core + near + far + row_bits, core + row_bits + far + near


def pick(even, odd):
    core = lax.axis_index("row") % 2
    device = {"row": lax.axis_index("row"), "col": lax.axis_index("col")}
    bit = 0
    for (axis, place), weight in ((even, 1 - core), (odd, core)):
        step, value = bit_of(axis, place)
        device[axis] = device[axis] + weight * step[axis]
        bit = bit + weight * value
    return (device["row"], device["col"]), bit


def sum_kernel(
    rows, cols, slab, sketch, total_ref, sampled_ref, inverse_ref,
    staged, sk, high, low, part, landed, left, grams, gram_in, work, wide_acc, slab_sem, sk_sem,
    send_sem, recv_sem, gram_send, gram_recv,
):
    height, width = slab.shape
    bits = (rows * cols).bit_length() - 1
    units = width // LANES * (LANES // TILE)
    chunk_units = units // CHUNKS
    chunk_cols = width // CHUNKS
    loads = width // LOAD

    sketch_copy = pltpu.make_async_copy(sketch, sk, sk_sem)
    sketch_copy.start()

    def load(i):
        return pltpu.make_async_copy(
            slab.at[:, pl.ds(pl.multiple_of(i * LOAD, LOAD), LOAD)], staged.at[i], slab_sem.at[i]
        )

    for i in range(loads):
        load(i).start()

    orders = [chunk_order(k, rows, cols) for k in range(CHUNKS)]
    gram_order = [("row", 0)] + [b for b in orders[0][0] if b != ("row", 0)]
    barrier = pltpu.get_barrier_semaphore()
    for place in gram_order:
        device, _ = pick(place, place)
        pl.semaphore_signal(barrier, inc=1, device_id=device, device_id_type=MESH)

    wide_acc[...] = jnp.zeros_like(wide_acc)
    sketch_copy.wait()

    def sample(i, carry):
        load(i).wait()
        a_high, a_low = split(staged[i])
        columns = pl.ds(pl.multiple_of(i * LOAD, LOAD), LOAD)
        high[:, columns] = a_high
        low[:, columns] = a_low
        s_high, s_low = split(sk[columns, :])
        both = jnp.concatenate([s_high, s_low], axis=1)
        wide_acc[...] += jnp.dot(a_high, both, preferred_element_type=F32)
        wide_acc[:, :LANES] += jnp.dot(a_low, s_high, preferred_element_type=F32)
        return carry

    lax.fori_loop(0, loads, sample, 0)
    sampled = wide_acc[:, :LANES] + wide_acc[:, LANES:]
    sampled_ref[...] = sampled
    turned = sampled.T
    t_high, t_low = split(turned)
    left[:LANES, :] = t_high
    left[LANES:, :] = t_low
    grams[0] = jnp.dot(
        turned, sampled, precision=lax.Precision.HIGHEST, preferred_element_type=F32
    )
    pl.semaphore_wait(barrier, bits)

    def product(k):
        def body(i, carry):
            start = pl.multiple_of(k * chunk_cols + i * WIDE, WIDE)
            b_high = high[:, pl.ds(start, WIDE)]
            both = jnp.dot(left[...], b_high, preferred_element_type=F32)
            more = jnp.dot(left[:LANES, :], low[:, pl.ds(start, WIDE)], preferred_element_type=F32)
            value = both[:LANES] + both[LANES:] + more
            per = LANES // TILE
            first = (k * chunk_cols // LANES + i * (WIDE // LANES)) * per
            for j in range(WIDE // LANES):
                part[pl.ds(first + j * per, per)] = value[:, j * LANES : (j + 1) * LANES].reshape(
                    per, TILE, LANES
                )
            return carry

        lax.fori_loop(0, chunk_cols // WIDE, body, 0)

    plan = []
    for k in range(CHUNKS):
        start, size, steps = k * chunk_units, chunk_units, []
        for even, odd in zip(*orders[k]):
            device, bit = pick(even, odd)
            half = size // 2
            keep, give = start + bit * half, start + (1 - bit) * half
            steps.append((device, keep, give, half, k * chunk_units + chunk_units - size))
            start, size = keep, half
        plan.append(steps)

    def scatter(k, s):
        device, _, give, half, slot = plan[k][s]
        return pltpu.make_async_remote_copy(
            src_ref=part.at[pl.ds(give, half)],
            dst_ref=landed.at[pl.ds(slot, half)],
            send_sem=send_sem.at[k, s],
            recv_sem=recv_sem.at[k, s],
            device_id=device,
            device_id_type=MESH,
        )

    def gather(k, s):
        device, keep, _, half, _ = plan[k][s]
        return pltpu.make_async_remote_copy(
            src_ref=total_ref.at[pl.ds(keep, half)],
            dst_ref=total_ref.at[pl.ds(keep, half)],
            send_sem=send_sem.at[k, 2 * bits - 1 - s],
            recv_sem=recv_sem.at[k, 2 * bits - 1 - s],
            device_id=device,
            device_id_type=MESH,
        )

    def exchange_gram(s):
        device, _ = pick(gram_order[s], gram_order[s])
        return pltpu.make_async_remote_copy(
            src_ref=grams.at[s],
            dst_ref=gram_in.at[s],
            send_sem=gram_send.at[s],
            recv_sem=gram_recv.at[s],
            device_id=device,
            device_id_type=MESH,
        )

    def chunk_step(k, s):
        if s == 0:
            product(k)
            scatter(k, 0).start()
        elif s <= bits:
            scatter(k, s - 1).wait_recv()
            _, keep, _, half, slot = plan[k][s - 1]
            value = part[pl.ds(keep, half)] + landed[pl.ds(slot, half)]
            if s < bits:
                part[pl.ds(keep, half)] = value
                scatter(k, s).start()
            else:
                total_ref[pl.ds(keep, half)] = value
                gather(k, bits - 1).start()
        else:
            gather(k, 2 * bits - s).wait_recv()
            if s < 2 * bits:
                gather(k, 2 * bits - s - 1).start()

    def gram_step(t):
        if 1 <= t <= bits:
            exchange_gram(t - 1).wait_recv()
            grams[t] = grams[t - 1] + gram_in[t - 1]
        if t < bits:
            exchange_gram(t).start()
        if t == bits:
            work[:, :LANES] = grams[bits]
            work[:, LANES:] = (
                lax.broadcasted_iota(jnp.int32, (LANES, LANES), 0)
                == lax.broadcasted_iota(jnp.int32, (LANES, LANES), 1)
            ).astype(F32)
        first = (t - bits - 1) * CHOL
        if 0 <= first < LANES:
            eliminate(first)

    def eliminate(first):
        lane = lax.broadcasted_iota(jnp.int32, (LANES, LANES), 1)
        sub = lax.broadcasted_iota(jnp.int32, (LANES, 1), 0)

        def body(j, carry):
            all_rows = work[...]
            column = jnp.sum(jnp.where(lane == j, all_rows[:, :LANES], 0.0), axis=1, keepdims=True)
            row = work[pl.ds(j, 1), :]
            pivot = jnp.sum(jnp.where(sub == j, column, 0.0), axis=0, keepdims=True)
            scale = 1.0 / jnp.sqrt(pivot)
            row = row * scale
            below = jnp.where(sub > j, column * scale, 0.0)
            work[...] = jnp.where(sub == j, row, all_rows - below * row)
            return carry

        lax.fori_loop(first, first + CHOL, body, 0)

    for t in range(max(CHUNKS + 2 * bits, bits + 1 + LANES // CHOL)):
        gram_step(t)
        for k in range(CHUNKS):
            if 0 <= t - k <= 2 * bits:
                chunk_step(k, t - k)

    inverse_ref[...] = work[:, LANES:]
    for k in range(CHUNKS):
        for s in range(bits):
            scatter(k, s).wait_send()
            gather(k, s).wait_send()
    for s in range(bits):
        exchange_gram(s).wait_send()


def apply_kernel(scale, total_ref, sampled_ref, inverse_ref, basis_ref, projection_ref):
    highest = lax.Precision.HIGHEST
    inverse = inverse_ref[...]

    @pl.when(pl.program_id(0) == 0)
    def _():
        turned = lax.dot_general(
            sampled_ref[...], inverse, (((1,), (1,)), ((), ())),
            precision=highest, preferred_element_type=F32,
        )
        basis_ref[...] = turned * scale

    per = LANES // TILE
    blocks = total_ref.shape[0] // per
    value = jnp.concatenate(
        [total_ref[b * per : (b + 1) * per].reshape(LANES, LANES) for b in range(blocks)], axis=1
    )
    projection_ref[...] = jnp.dot(inverse, value, precision=highest, preferred_element_type=F32)


def per_device(rows, cols, slab, sketch):
    height, width = slab.shape
    rank = sketch.shape[1]
    bits = (rows * cols).bit_length() - 1
    units = width // LANES * (rank // TILE)
    vmem = pl.BlockSpec(memory_space=pltpu.VMEM)
    total, sampled, inverse = pl.pallas_call(
        functools.partial(sum_kernel, rows, cols),
        out_shape=(
            jax.ShapeDtypeStruct((units, TILE, LANES), F32),
            jax.ShapeDtypeStruct((height, rank), F32),
            jax.ShapeDtypeStruct((rank, rank), F32),
        ),
        in_specs=[pl.BlockSpec(memory_space=pl.ANY)] * 2,
        out_specs=(vmem, vmem, vmem),
        scratch_shapes=[
            pltpu.VMEM((width // LOAD, height, LOAD), F32),
            pltpu.VMEM((width, rank), F32),
            pltpu.VMEM((height, width), BF16),
            pltpu.VMEM((height, width), BF16),
            pltpu.VMEM((units, TILE, LANES), F32),
            pltpu.VMEM((units, TILE, LANES), F32),
            pltpu.VMEM((2 * rank, height), BF16),
            pltpu.VMEM((bits + 1, rank, rank), F32),
            pltpu.VMEM((bits, rank, rank), F32),
            pltpu.VMEM((rank, 2 * rank), F32),
            pltpu.VMEM((height, 2 * rank), F32),
            pltpu.SemaphoreType.DMA((width // LOAD,)),
            pltpu.SemaphoreType.DMA,
            pltpu.SemaphoreType.DMA((CHUNKS, 2 * bits)),
            pltpu.SemaphoreType.DMA((CHUNKS, 2 * bits)),
            pltpu.SemaphoreType.DMA((bits,)),
            pltpu.SemaphoreType.DMA((bits,)),
        ],
        compiler_params=pltpu.CompilerParams(
            collective_id=0, has_side_effects=True, vmem_limit_bytes=56 * 2**20
        ),
    )(slab, sketch)
    pieces = 8
    whole = lambda shape: pl.BlockSpec(shape, lambda i: (0,) * len(shape))
    return pl.pallas_call(
        functools.partial(apply_kernel, math.sqrt(height * rows * cols)),
        grid=(pieces,),
        out_shape=(
            jax.ShapeDtypeStruct((height, rank), F32),
            jax.ShapeDtypeStruct((rank, width), F32),
        ),
        in_specs=[
            pl.BlockSpec((units // pieces, TILE, LANES), lambda i: (i, 0, 0)),
            whole((height, rank)),
            whole((rank, rank)),
        ],
        out_specs=(whole((height, rank)), pl.BlockSpec((rank, width // pieces), lambda i: (0, i))),
        compiler_params=pltpu.CompilerParams(vmem_limit_bytes=16 * 2**20),
    )(total, sampled, inverse)


def solution(mesh):
    rows, cols = mesh.shape["row"], mesh.shape["col"]
    placed = (P(("row", "col"), None), P())
    return jax.shard_map(
        functools.partial(per_device, rows, cols),
        mesh=mesh,
        in_specs=placed,
        out_specs=placed,
        check_vma=False,
    )
```

```python
import functools
import math

import jax
import jax.numpy as jnp
from jax import lax
from jax.experimental import pallas as pl
from jax.experimental.pallas import tpu as pltpu
from jax.sharding import PartitionSpec as P

MESH = pl.DeviceIdType.MESH
BF16 = jnp.bfloat16
F32 = jnp.float32
LANES = 128
TILE = 8
LOAD = 512
WIDE = 256
MOST_CHUNKS = 16
HOP = 2
PANEL = 32
CHOL = 8


def split(value):
    high = value.astype(BF16)
    return high, (value - high.astype(F32)).astype(BF16)


def bit_of(axis, bit):
    index = lax.axis_index(axis)
    value = (index // 2**bit) % 2
    return {axis: 2**bit * (1 - 2 * value)}, value


def chunk_order(chunk, rows, cols):
    row_bits = [("row", b) for b in range(1, rows.bit_length() - 1)]
    col_bits = [("col", b) for b in range(cols.bit_length() - 1)]
    inner = 1 if len(col_bits) == 3 else len(col_bits) // 2
    near, far = col_bits[:inner], col_bits[inner:]
    core = [("row", 0)]
    if chunk % 3 == 2:
        return core + near + row_bits + far, core + row_bits + near + far
    return core + near + far + row_bits, core + row_bits + far + near


def pick(even, odd):
    core = lax.axis_index("row") % 2
    device = {"row": lax.axis_index("row"), "col": lax.axis_index("col")}
    bit = 0
    for (axis, place), weight in ((even, 1 - core), (odd, core)):
        step, value = bit_of(axis, place)
        device[axis] = device[axis] + weight * step[axis]
        bit = bit + weight * value
    return (device["row"], device["col"]), bit


def sum_kernel(
    rows, cols, slab, sketch, total_out, sampled_out, inverse_out,
    staged, sk, high, low, part, landed, total_ref, sampled_ref, inverse_ref, left, grams, gram_in,
    work, panel, wide_acc, slab_sem, sk_sem, send_sem, recv_sem, gram_send, gram_recv, total_sem,
    out_sem,
):
    height, width = slab.shape
    bits = (rows * cols).bit_length() - 1
    units = width // LANES * (LANES // TILE)
    chunks = min(MOST_CHUNKS, units >> bits)
    chunk_units = units // chunks
    chunk_cols = width // chunks
    loads = width // LOAD

    sketch_copy = pltpu.make_async_copy(sketch, sk, sk_sem)
    sketch_copy.start()

    def load(i):
        return pltpu.make_async_copy(
            slab.at[:, pl.ds(pl.multiple_of(i * LOAD, LOAD), LOAD)], staged.at[i], slab_sem.at[i]
        )

    for i in range(loads):
        load(i).start()

    orders = [chunk_order(k, rows, cols) for k in range(chunks)]
    gram_order = [("row", 0)] + [b for b in orders[0][0] if b != ("row", 0)]
    barrier = pltpu.get_barrier_semaphore()
    for place in gram_order:
        device, _ = pick(place, place)
        pl.semaphore_signal(barrier, inc=1, device_id=device, device_id_type=MESH)

    wide_acc[...] = jnp.zeros_like(wide_acc)
    sketch_copy.wait()

    def sample(i, carry):
        load(i).wait()
        a_high, a_low = split(staged[i])
        columns = pl.ds(pl.multiple_of(i * LOAD, LOAD), LOAD)
        high[:, columns] = a_high
        low[:, columns] = a_low
        s_high, s_low = split(sk[columns, :])
        both = jnp.concatenate([s_high, s_low], axis=1)
        wide_acc[...] += jnp.dot(a_high, both, preferred_element_type=F32)
        wide_acc[:, :LANES] += jnp.dot(a_low, s_high, preferred_element_type=F32)
        return carry

    lax.fori_loop(0, loads, sample, 0)
    sampled = wide_acc[:, :LANES] + wide_acc[:, LANES:]
    sampled_ref[...] = sampled
    sampled_copy = pltpu.make_async_copy(sampled_ref, sampled_out, out_sem.at[0])
    sampled_copy.start()
    turned = sampled.T
    t_high, t_low = split(turned)
    left[:LANES, :] = t_high
    left[LANES:, :] = t_low
    grams[0] = jnp.dot(
        turned, sampled, precision=lax.Precision.HIGHEST, preferred_element_type=F32
    )
    pl.semaphore_wait(barrier, bits)

    def product(k):
        def body(i, carry):
            start = pl.multiple_of(k * chunk_cols + i * WIDE, WIDE)
            b_high = high[:, pl.ds(start, WIDE)]
            both = jnp.dot(left[...], b_high, preferred_element_type=F32)
            more = jnp.dot(left[:LANES, :], low[:, pl.ds(start, WIDE)], preferred_element_type=F32)
            value = both[:LANES] + both[LANES:] + more
            per = LANES // TILE
            first = (k * chunk_cols // LANES + i * (WIDE // LANES)) * per
            for j in range(WIDE // LANES):
                part[pl.ds(first + j * per, per)] = value[:, j * LANES : (j + 1) * LANES].reshape(
                    per, TILE, LANES
                )
            return carry

        lax.fori_loop(0, chunk_cols // WIDE, body, 0)

    plan = []
    for k in range(chunks):
        start, size, steps = k * chunk_units, chunk_units, []
        for even, odd in zip(*orders[k]):
            device, bit = pick(even, odd)
            half = size // 2
            keep, give = start + bit * half, start + (1 - bit) * half
            steps.append((device, keep, give, half, k * chunk_units + chunk_units - size))
            start, size = keep, half
        plan.append(steps)

    def scatter(k, s):
        device, _, give, half, slot = plan[k][s]
        return pltpu.make_async_remote_copy(
            src_ref=part.at[pl.ds(give, half)],
            dst_ref=landed.at[pl.ds(slot, half)],
            send_sem=send_sem.at[k, s],
            recv_sem=recv_sem.at[k, s],
            device_id=device,
            device_id_type=MESH,
        )

    def gather(k, s):
        device, keep, _, half, _ = plan[k][s]
        return pltpu.make_async_remote_copy(
            src_ref=total_ref.at[pl.ds(keep, half)],
            dst_ref=total_ref.at[pl.ds(keep, half)],
            send_sem=send_sem.at[k, 2 * bits - 1 - s],
            recv_sem=recv_sem.at[k, 2 * bits - 1 - s],
            device_id=device,
            device_id_type=MESH,
        )

    def exchange_gram(s):
        device, _ = pick(gram_order[s], gram_order[s])
        return pltpu.make_async_remote_copy(
            src_ref=grams.at[s],
            dst_ref=gram_in.at[s],
            send_sem=gram_send.at[s],
            recv_sem=gram_recv.at[s],
            device_id=device,
            device_id_type=MESH,
        )

    def deliver(k):
        region = pl.ds(k * chunk_units, chunk_units)
        return pltpu.make_async_copy(total_ref.at[region], total_out.at[region], total_sem.at[k])

    def chunk_step(k, s):
        if s == 0:
            product(k)
            scatter(k, 0).start()
        elif s <= bits:
            scatter(k, s - 1).wait_recv()
            _, keep, _, half, slot = plan[k][s - 1]
            value = part[pl.ds(keep, half)] + landed[pl.ds(slot, half)]
            if s < bits:
                part[pl.ds(keep, half)] = value
                scatter(k, s).start()
            else:
                total_ref[pl.ds(keep, half)] = value
                gather(k, bits - 1).start()
        else:
            gather(k, 2 * bits - s).wait_recv()
            if s < 2 * bits:
                gather(k, 2 * bits - s - 1).start()
            else:
                deliver(k).start()

    def gram_step(t):
        step = t // HOP
        if t % HOP == 0:
            if 1 <= step <= bits:
                exchange_gram(step - 1).wait_recv()
                grams[step] = grams[step - 1] + gram_in[step - 1]
            if step < bits:
                exchange_gram(step).start()
            if step == bits:
                work[:, :LANES] = grams[bits]
                work[:, LANES:] = (square_rows == square_lanes).astype(F32)
        first = (t - HOP * bits - 1) * CHOL
        if 0 <= first < LANES:
            eliminate(first)

    square_rows = lax.broadcasted_iota(jnp.int32, (LANES, LANES), 0)
    square_lanes = lax.broadcasted_iota(jnp.int32, (LANES, LANES), 1)
    panel_rows = lax.broadcasted_iota(jnp.int32, (PANEL, LANES), 0)
    panel_lanes = lax.broadcasted_iota(jnp.int32, (PANEL, LANES), 1)

    def eliminate(first):
        base = first // PANEL * PANEL
        here = pl.ds(base, PANEL)
        if first == base:
            block = work[here, :LANES]
            if base:
                block = pltpu.roll(block, LANES - base, 1)
            unit = (panel_rows + PANEL == panel_lanes).astype(F32)
            value = jnp.where(panel_lanes < PANEL, block, unit)
        else:
            value = panel[...]
        for j in range(first - base, first - base + CHOL):
            ratio = value[:, j : j + 1] / value[j : j + 1, j : j + 1]
            below = jnp.where(panel_rows > j, ratio, 0.0)
            value = value - below * value[j : j + 1, :]
        panel[...] = value
        if first + CHOL < base + PANEL:
            return
        diagonal = jnp.sum(
            jnp.where(panel_rows == panel_lanes, value, 0.0), axis=1, keepdims=True
        )
        value = value / jnp.sqrt(diagonal)
        shift = (base - PANEL) % LANES
        if shift:
            value = pltpu.roll(value, shift, 1)
        inside = jnp.logical_and(panel_lanes >= base, panel_lanes < base + PANEL)
        value = jnp.where(inside, value, 0.0)
        highest = lax.Precision.HIGHEST
        done = jnp.dot(value, work[...], precision=highest, preferred_element_type=F32)
        work[here, :] = done
        if base + PANEL < LANES:
            change = jnp.dot(done[:, :LANES].T, done, precision=highest, preferred_element_type=F32)
            rest = slice(base + PANEL, LANES)
            work[rest, :] = work[rest, :] - change[rest, :]
        else:
            inverse_ref[...] = work[:, LANES:]
            pltpu.make_async_copy(inverse_ref, inverse_out, out_sem.at[1]).start()

    for t in range(max(chunks + HOP * 2 * bits, HOP * bits + 1 + LANES // CHOL)):
        gram_step(t)
        for k in range(chunks):
            if t >= k and (t - k) % HOP == 0 and (t - k) // HOP <= 2 * bits:
                chunk_step(k, (t - k) // HOP)

    sampled_copy.wait()
    pltpu.make_async_copy(inverse_ref, inverse_out, out_sem.at[1]).wait()
    for k in range(chunks):
        deliver(k).wait()
        for s in range(bits):
            scatter(k, s).wait_send()
            gather(k, s).wait_send()
    for s in range(bits):
        exchange_gram(s).wait_send()


def apply_kernel(scale, total_ref, sampled_ref, inverse_ref, basis_ref, projection_ref):
    highest = lax.Precision.HIGHEST
    inverse = inverse_ref[...]

    @pl.when(pl.program_id(0) == 0)
    def _():
        turned = lax.dot_general(
            sampled_ref[...], inverse, (((1,), (1,)), ((), ())),
            precision=highest, preferred_element_type=F32,
        )
        basis_ref[...] = turned * scale

    per = LANES // TILE
    blocks = total_ref.shape[0] // per
    value = jnp.concatenate(
        [total_ref[b * per : (b + 1) * per].reshape(LANES, LANES) for b in range(blocks)], axis=1
    )
    v_high, v_low = split(value)
    i_high, i_low = split(inverse)
    projection_ref[...] = jnp.dot(
        jnp.concatenate([i_high, i_high], axis=1),
        jnp.concatenate([v_high, v_low], axis=0),
        preferred_element_type=F32,
    ) + jnp.dot(i_low, v_high, preferred_element_type=F32)


def per_device(rows, cols, slab, sketch):
    height, width = slab.shape
    rank = sketch.shape[1]
    bits = (rows * cols).bit_length() - 1
    units = width // LANES * (rank // TILE)
    chunks = min(MOST_CHUNKS, units >> bits)
    anywhere = pl.BlockSpec(memory_space=pl.ANY)
    total, sampled, inverse = pl.pallas_call(
        functools.partial(sum_kernel, rows, cols),
        out_shape=(
            jax.ShapeDtypeStruct((units, TILE, LANES), F32),
            jax.ShapeDtypeStruct((height, rank), F32),
            jax.ShapeDtypeStruct((rank, rank), F32),
        ),
        in_specs=[anywhere] * 2,
        out_specs=(anywhere,) * 3,
        scratch_shapes=[
            pltpu.VMEM((width // LOAD, height, LOAD), F32),
            pltpu.VMEM((width, rank), F32),
            pltpu.VMEM((height, width), BF16),
            pltpu.VMEM((height, width), BF16),
            pltpu.VMEM((units, TILE, LANES), F32),
            pltpu.VMEM((units, TILE, LANES), F32),
            pltpu.VMEM((units, TILE, LANES), F32),
            pltpu.VMEM((height, rank), F32),
            pltpu.VMEM((rank, rank), F32),
            pltpu.VMEM((2 * rank, height), BF16),
            pltpu.VMEM((bits + 1, rank, rank), F32),
            pltpu.VMEM((bits, rank, rank), F32),
            pltpu.VMEM((rank, 2 * rank), F32),
            pltpu.VMEM((PANEL, rank), F32),
            pltpu.VMEM((height, 2 * rank), F32),
            pltpu.SemaphoreType.DMA((width // LOAD,)),
            pltpu.SemaphoreType.DMA,
            pltpu.SemaphoreType.DMA((chunks, 2 * bits)),
            pltpu.SemaphoreType.DMA((chunks, 2 * bits)),
            pltpu.SemaphoreType.DMA((bits,)),
            pltpu.SemaphoreType.DMA((bits,)),
            pltpu.SemaphoreType.DMA((chunks,)),
            pltpu.SemaphoreType.DMA((2,)),
        ],
        compiler_params=pltpu.CompilerParams(
            collective_id=0, has_side_effects=True, vmem_limit_bytes=56 * 2**20
        ),
    )(slab, sketch)
    pieces = 8
    whole = lambda shape: pl.BlockSpec(shape, lambda i: (0,) * len(shape))
    return pl.pallas_call(
        functools.partial(apply_kernel, math.sqrt(height * rows * cols)),
        grid=(pieces,),
        out_shape=(
            jax.ShapeDtypeStruct((height, rank), F32),
            jax.ShapeDtypeStruct((rank, width), F32),
        ),
        in_specs=[
            pl.BlockSpec((units // pieces, TILE, LANES), lambda i: (i, 0, 0)),
            whole((height, rank)),
            whole((rank, rank)),
        ],
        out_specs=(whole((height, rank)), pl.BlockSpec((rank, width // pieces), lambda i: (0, i))),
        compiler_params=pltpu.CompilerParams(vmem_limit_bytes=56 * 2**20),
    )(total, sampled, inverse)


def solution(mesh):
    rows, cols = mesh.shape["row"], mesh.shape["col"]
    placed = (P(("row", "col"), None), P())
    return jax.shard_map(
        functools.partial(per_device, rows, cols),
        mesh=mesh,
        in_specs=placed,
        out_specs=placed,
        check_vma=False,
    )
```

```python
import functools
import math

import jax
import jax.numpy as jnp
from jax import lax
from jax.experimental import pallas as pl
from jax.experimental.pallas import tpu as pltpu
from jax.sharding import PartitionSpec as P

MESH = pl.DeviceIdType.MESH
BF16 = jnp.bfloat16
F32 = jnp.float32
LANES = 128
TILE = 8
LOAD = 512
MOST_CHUNKS = 16
HOP = 2
PANEL = 32
CHOL = 16


def split(value):
    high = value.astype(BF16)
    return high, (value - high.astype(F32)).astype(BF16)


def bit_of(axis, bit):
    index = lax.axis_index(axis)
    value = (index // 2**bit) % 2
    return {axis: 2**bit * (1 - 2 * value)}, value


def orders(rows, cols):
    row_bits = [("row", b) for b in range(1, rows.bit_length() - 1)]
    col_bits = [("col", b) for b in range(cols.bit_length() - 1)]
    inner = 1 if len(col_bits) == 3 else len(col_bits) // 2
    near, far = col_bits[:inner], col_bits[inner:]
    core = [("row", 0)]
    return (
        (core + near + far + row_bits, core + row_bits + far + near),
        (core + near + row_bits + far, core + row_bits + near + far),
    )


def pick(even, odd):
    core = lax.axis_index("row") % 2
    device = {"row": lax.axis_index("row"), "col": lax.axis_index("col")}
    bit = 0
    for (axis, place), weight in ((even, 1 - core), (odd, core)):
        step, value = bit_of(axis, place)
        device[axis] = device[axis] + weight * step[axis]
        bit = bit + weight * value
    return (device["row"], device["col"]), bit


def sum_kernel(
    rows, cols, slab, sketch, basis_out, projection_out,
    staged, sk, high, low, part, landed, total, basis, left, grams, gram_in, work, panel, wide_acc,
    slab_sem, sk_sem, send_sem, recv_sem, gram_send, gram_recv, out_sem, basis_sem,
):
    height, width = slab.shape
    bits = (rows * cols).bit_length() - 1
    units = width // LANES * (LANES // TILE)
    chunks = min(MOST_CHUNKS, units >> bits)
    chunk_units = units // chunks
    chunk_cols = width // chunks
    loads = width // LOAD

    sketch_copy = pltpu.make_async_copy(sketch, sk, sk_sem)
    sketch_copy.start()

    def load(i):
        return pltpu.make_async_copy(
            slab.at[:, pl.ds(pl.multiple_of(i * LOAD, LOAD), LOAD)], staged.at[i], slab_sem.at[i]
        )

    for i in range(loads):
        load(i).start()

    plans = orders(rows, cols)
    gram_order = plans[0][0]
    barrier = pltpu.get_barrier_semaphore()
    for place in gram_order:
        device, _ = pick(place, place)
        pl.semaphore_signal(barrier, inc=1, device_id=device, device_id_type=MESH)

    wide_acc[...] = jnp.zeros_like(wide_acc)
    sketch_copy.wait()

    def sample(i, carry):
        load(i).wait()
        a_high, a_low = split(staged[i])
        columns = pl.ds(pl.multiple_of(i * LOAD, LOAD), LOAD)
        high[:, columns] = a_high
        low[:, columns] = a_low
        s_high, s_low = split(sk[columns, :])
        both = jnp.concatenate([s_high, s_low], axis=1)
        wide_acc[...] += jnp.dot(a_high, both, preferred_element_type=F32)
        wide_acc[:, :LANES] += jnp.dot(a_low, s_high, preferred_element_type=F32)
        return carry

    lax.fori_loop(0, loads, sample, 0)
    sampled = wide_acc[:, :LANES] + wide_acc[:, LANES:]
    basis[...] = sampled
    turned = sampled.T
    t_high, t_low = split(turned)
    left[:LANES, :] = t_high
    left[LANES:, :] = t_low
    grams[0] = jnp.dot(
        turned, sampled, precision=lax.Precision.HIGHEST, preferred_element_type=F32
    )
    pl.semaphore_wait(barrier, bits)

    per = LANES // TILE
    strips = chunk_cols // LOAD

    def product(k):
        for i in range(strips):
            columns = pl.ds(pl.multiple_of((k * strips + i) * LOAD, LOAD), LOAD)
            both = jnp.dot(left[...], high[:, columns], preferred_element_type=F32)
            more = jnp.dot(left[:LANES, :], low[:, columns], preferred_element_type=F32)
            value = both[:LANES] + both[LANES:] + more
            for j in range(LOAD // LANES):
                first = k * chunk_units + (i * (LOAD // LANES) + j) * per
                part[pl.ds(first, per)] = value[:, j * LANES : (j + 1) * LANES].reshape(
                    per, TILE, LANES
                )

    tables = []
    for even, odd in plans:
        start, size, steps = 0, chunk_units, []
        for step_even, step_odd in zip(even, odd):
            device, bit = pick(step_even, step_odd)
            half = size // 2
            steps.append((*device, start + bit * half, start + (1 - bit) * half))
            start, size = start + bit * half, half
        tables.append(steps)

    def place(k, s):
        second = (k % 3) // 2
        row, col, keep, give = (
            a + second * (b - a) for a, b in zip(tables[0][s], tables[1][s])
        )
        half = chunk_units >> (s + 1)
        base = k * chunk_units
        return (row, col), base + keep, base + give, half, base + chunk_units - 2 * half

    def scatter(k, s):
        device, _, give, half, slot = place(k, s)
        return pltpu.make_async_remote_copy(
            src_ref=part.at[pl.ds(give, half)],
            dst_ref=landed.at[pl.ds(slot, half)],
            send_sem=send_sem.at[k, s],
            recv_sem=recv_sem.at[k, s],
            device_id=device,
            device_id_type=MESH,
        )

    def gather(k, s):
        device, keep, _, half, _ = place(k, s)
        return pltpu.make_async_remote_copy(
            src_ref=total.at[pl.ds(keep, half)],
            dst_ref=total.at[pl.ds(keep, half)],
            send_sem=send_sem.at[k, 2 * bits - 1 - s],
            recv_sem=recv_sem.at[k, 2 * bits - 1 - s],
            device_id=device,
            device_id_type=MESH,
        )

    def exchange_gram(s):
        device, _ = pick(gram_order[s], gram_order[s])
        return pltpu.make_async_remote_copy(
            src_ref=grams.at[s],
            dst_ref=gram_in.at[s],
            send_sem=gram_send.at[s],
            recv_sem=gram_recv.at[s],
            device_id=device,
            device_id_type=MESH,
        )

    def deliver(strip):
        return pltpu.make_async_copy(
            staged.at[strip, pl.ds(0, LANES)],
            projection_out.at[:, pl.ds(pl.multiple_of(strip * LOAD, LOAD), LOAD)],
            out_sem.at[strip],
        )

    def apply(k):
        inverse = work[:, LANES:]
        i_high, i_low = split(inverse)
        doubled = jnp.concatenate([i_high, i_high], axis=1)
        for i in range(strips):
            first = k * chunk_units + i * (LOAD // LANES) * per
            value = jnp.concatenate(
                [
                    total[pl.ds(first + j * per, per)].reshape(LANES, LANES)
                    for j in range(LOAD // LANES)
                ],
                axis=1,
            )
            v_high, v_low = split(value)
            strip = k * strips + i
            staged[strip, :LANES, :] = jnp.dot(
                doubled, jnp.concatenate([v_high, v_low], axis=0), preferred_element_type=F32
            ) + jnp.dot(i_low, v_high, preferred_element_type=F32)
            deliver(strip).start()

    def chunk_step(k, s):
        if s == 0:
            product(k)
            scatter(k, 0).start()
        elif s <= bits:
            scatter(k, s - 1).wait_recv()
            _, keep, _, half, slot = place(k, s - 1)
            value = part[pl.ds(keep, half)] + landed[pl.ds(slot, half)]
            if s < bits:
                part[pl.ds(keep, half)] = value
                scatter(k, s).start()
            else:
                total[pl.ds(keep, half)] = value
                gather(k, bits - 1).start()
        else:
            gather(k, 2 * bits - s).wait_recv()
            if s < 2 * bits:
                gather(k, 2 * bits - s - 1).start()
            else:
                apply(k)

    square_rows = lax.broadcasted_iota(jnp.int32, (LANES, LANES), 0)
    square_lanes = lax.broadcasted_iota(jnp.int32, (LANES, LANES), 1)
    panel_rows = lax.broadcasted_iota(jnp.int32, (PANEL, LANES), 0)
    panel_lanes = lax.broadcasted_iota(jnp.int32, (PANEL, LANES), 1)
    highest = lax.Precision.HIGHEST
    basis_copy = pltpu.make_async_copy(basis, basis_out, basis_sem)

    def gram_step(step):
        if step >= 1:
            exchange_gram(step - 1).wait_recv()
            grams[step] = grams[step - 1] + gram_in[step - 1]
        if step < bits:
            exchange_gram(step).start()
        else:
            work[:, :LANES] = grams[bits]
            work[:, LANES:] = (square_rows == square_lanes).astype(F32)

    def eliminate(base, piece):
        here = pl.ds(pl.multiple_of(base, PANEL), PANEL)
        if piece == 0:
            block = pltpu.roll(work[here, :LANES], (LANES - base) % LANES, 1)
            unit = (panel_rows + PANEL == panel_lanes).astype(F32)
            value = jnp.where(panel_lanes < PANEL, block, unit)
        else:
            value = panel[...]
        for j in range(piece * CHOL, (piece + 1) * CHOL):
            column = jnp.broadcast_to(value[:, j : j + 1], (PANEL, LANES))
            row = value[j : j + 1, :] / column[j : j + 1, :]
            value = value - jnp.where(panel_rows > j, column, 0.0) * row
        panel[...] = value
        if (piece + 1) * CHOL < PANEL:
            return
        diagonal = jnp.sum(
            jnp.where(panel_rows == panel_lanes, value, 0.0), axis=1, keepdims=True
        )
        value = pltpu.roll(value / jnp.sqrt(diagonal), (base + LANES - PANEL) % LANES, 1)
        inside = jnp.logical_and(panel_lanes >= base, panel_lanes < base + PANEL)
        value = jnp.where(inside, value, 0.0)
        done = jnp.dot(value, work[...], precision=highest, preferred_element_type=F32)
        work[here, :] = done
        change = jnp.dot(done[:, :LANES].T, done, precision=highest, preferred_element_type=F32)
        rest = lax.broadcasted_iota(jnp.int32, (LANES, 2 * LANES), 0) >= base + PANEL
        work[...] = jnp.where(rest, work[...] - change, work[...])

    def make_basis():
        product_turned = lax.dot_general(
            basis[...], work[:, LANES:], (((1,), (1,)), ((), ())),
            precision=highest, preferred_element_type=F32,
        )
        basis[...] = product_turned * math.sqrt(height * rows * cols)
        basis_copy.start()

    first_elimination = HOP * bits + 1
    pieces = PANEL // CHOL

    def tick(t, carry):
        for step in range(bits + 1):
            pl.when(t == HOP * step)(functools.partial(gram_step, step))
        for s in reversed(range(2 * bits + 1)):
            k = t - HOP * s
            pl.when(jnp.logical_and(k >= 0, k < chunks))(functools.partial(chunk_step, k, s))
        done = t - first_elimination
        for piece in range(pieces):
            due = jnp.logical_and(done >= 0, done < LANES // CHOL)
            base = done // pieces * PANEL
            pl.when(jnp.logical_and(due, done % pieces == piece))(
                functools.partial(eliminate, base, piece)
            )
        pl.when(done == LANES // CHOL)(make_basis)
        return carry

    lax.fori_loop(0, chunks + HOP * 2 * bits, tick, 0)

    def drain(k, carry):
        for s in range(bits):
            scatter(k, s).wait_send()
            gather(k, s).wait_send()
        for i in range(strips):
            deliver(k * strips + i).wait()
        return carry

    lax.fori_loop(0, chunks, drain, 0)
    basis_copy.wait()
    for s in range(bits):
        exchange_gram(s).wait_send()


def per_device(rows, cols, slab, sketch):
    height, width = slab.shape
    rank = sketch.shape[1]
    bits = (rows * cols).bit_length() - 1
    units = width // LANES * (rank // TILE)
    chunks = min(MOST_CHUNKS, units >> bits)
    anywhere = pl.BlockSpec(memory_space=pl.ANY)
    return pl.pallas_call(
        functools.partial(sum_kernel, rows, cols),
        out_shape=(
            jax.ShapeDtypeStruct((height, rank), F32),
            jax.ShapeDtypeStruct((rank, width), F32),
        ),
        in_specs=[anywhere] * 2,
        out_specs=(anywhere,) * 2,
        scratch_shapes=[
            pltpu.VMEM((width // LOAD, height, LOAD), F32),
            pltpu.VMEM((width, rank), F32),
            pltpu.VMEM((height, width), BF16),
            pltpu.VMEM((height, width), BF16),
            pltpu.VMEM((units, TILE, LANES), F32),
            pltpu.VMEM((units, TILE, LANES), F32),
            pltpu.VMEM((units, TILE, LANES), F32),
            pltpu.VMEM((height, rank), F32),
            pltpu.VMEM((2 * rank, height), BF16),
            pltpu.VMEM((bits + 1, rank, rank), F32),
            pltpu.VMEM((bits, rank, rank), F32),
            pltpu.VMEM((rank, 2 * rank), F32),
            pltpu.VMEM((PANEL, rank), F32),
            pltpu.VMEM((height, 2 * rank), F32),
            pltpu.SemaphoreType.DMA((width // LOAD,)),
            pltpu.SemaphoreType.DMA,
            pltpu.SemaphoreType.DMA((chunks, 2 * bits)),
            pltpu.SemaphoreType.DMA((chunks, 2 * bits)),
            pltpu.SemaphoreType.DMA((bits,)),
            pltpu.SemaphoreType.DMA((bits,)),
            pltpu.SemaphoreType.DMA((width // LOAD,)),
            pltpu.SemaphoreType.DMA,
        ],
        compiler_params=pltpu.CompilerParams(
            collective_id=0, has_side_effects=True, vmem_limit_bytes=56 * 2**20
        ),
    )(slab, sketch)


def solution(mesh):
    rows, cols = mesh.shape["row"], mesh.shape["col"]
    placed = (P(("row", "col"), None), P())
    return jax.shard_map(
        functools.partial(per_device, rows, cols),
        mesh=mesh,
        in_specs=placed,
        out_specs=placed,
        check_vma=False,
    )
```

```python
import functools
import math

import jax
import jax.numpy as jnp
from jax import lax
from jax.experimental import pallas as pl
from jax.experimental.pallas import tpu as pltpu
from jax.sharding import PartitionSpec as P

MESH = pl.DeviceIdType.MESH
BF16 = jnp.bfloat16
F32 = jnp.float32
LANES = 128
TILE = 8
LOAD = 1024
CHUNKS = 8
STRIP = 512
HOP = 2
PANEL = 32
CHOL = 16


def split(value):
    high = value.astype(BF16)
    return high, (value - high.astype(F32)).astype(BF16)


def bit_of(axis, bit):
    index = lax.axis_index(axis)
    value = (index // 2**bit) % 2
    return {axis: 2**bit * (1 - 2 * value)}, value


def orders(rows, cols):
    row_bits = [("row", b) for b in range(1, rows.bit_length() - 1)]
    col_bits = [("col", b) for b in range(cols.bit_length() - 1)]
    inner = 1 if len(col_bits) == 3 else len(col_bits) // 2
    near, far = col_bits[:inner], col_bits[inner:]
    core = [("row", 0)]
    return list(zip(core + near + row_bits, core + row_bits + near)), [(b, b) for b in far]


def pick(even, odd):
    core = lax.axis_index("row") % 2
    device = {"row": lax.axis_index("row"), "col": lax.axis_index("col")}
    bit = 0
    for (axis, place), weight in ((even, 1 - core), (odd, core)):
        step, value = bit_of(axis, place)
        device[axis] = device[axis] + weight * step[axis]
        bit = bit + weight * value
    return (device["row"], device["col"]), bit


def sum_kernel(
    rows, cols, slab, sketch, basis_out, projection_out,
    staged, sk, high, low, part, landed, total, swap_in, swap_out, basis, left, grams, gram_in, work, panel, wide_acc,
    slab_sem, sk_sem, send_sem, recv_sem, gram_send, gram_recv, out_sem, basis_sem,
):
    height, width = slab.shape
    bits = (rows * cols).bit_length() - 1
    units = width // LANES * (LANES // TILE)
    chunks = CHUNKS
    chunk_units = units // chunks
    chunk_cols = width // chunks
    loads = width // LOAD

    sketch_copy = pltpu.make_async_copy(sketch, sk, sk_sem)
    sketch_copy.start()

    def load(i):
        return pltpu.make_async_copy(
            slab.at[:, pl.ds(pl.multiple_of(i * LOAD, LOAD), LOAD)], staged.at[i], slab_sem.at[i]
        )

    for i in range(loads):
        load(i).start()

    halving, swapping = orders(rows, cols)
    halves, swaps = len(halving), len(swapping)
    kept_units = chunk_units >> halves
    gram_order = [(even, even) for even, _ in halving + swapping]
    barrier = pltpu.get_barrier_semaphore()
    for place in gram_order:
        device, _ = pick(*place)
        pl.semaphore_signal(barrier, inc=1, device_id=device, device_id_type=MESH)

    wide_acc[...] = jnp.zeros_like(wide_acc)
    sketch_copy.wait()

    def sample(i, carry):
        load(i).wait()
        a_high, a_low = split(staged[i])
        columns = pl.ds(pl.multiple_of(i * LOAD, LOAD), LOAD)
        high[:, columns] = a_high
        low[:, columns] = a_low
        s_high, s_low = split(sk[columns, :])
        both = jnp.concatenate([s_high, s_low], axis=1)
        wide_acc[...] += jnp.dot(a_high, both, preferred_element_type=F32)
        wide_acc[:, :LANES] += jnp.dot(a_low, s_high, preferred_element_type=F32)
        return carry

    lax.fori_loop(0, loads, sample, 0)
    sampled = wide_acc[:, :LANES] + wide_acc[:, LANES:]
    basis[...] = sampled
    turned = sampled.T
    t_high, t_low = split(turned)
    left[:LANES, :] = t_high
    left[LANES:, :] = t_low
    grams[0] = jnp.dot(
        turned, sampled, precision=lax.Precision.HIGHEST, preferred_element_type=F32
    )
    pl.semaphore_wait(barrier, bits)

    per = LANES // TILE
    strips = chunk_cols // STRIP

    def product(k):
        for i in range(strips):
            columns = pl.ds(pl.multiple_of((k * strips + i) * STRIP, STRIP), STRIP)
            both = jnp.dot(left[...], high[:, columns], preferred_element_type=F32)
            more = jnp.dot(left[:LANES, :], low[:, columns], preferred_element_type=F32)
            value = both[:LANES] + both[LANES:] + more
            for j in range(STRIP // LANES):
                first = k * chunk_units + (i * (STRIP // LANES) + j) * per
                part[pl.ds(first, per)] = value[:, j * LANES : (j + 1) * LANES].reshape(
                    per, TILE, LANES
                )

    table, start = [], 0
    for s, places in enumerate(halving):
        device, bit = pick(*places)
        half = chunk_units >> (s + 1)
        table.append((device, start + bit * half, start + (1 - bit) * half))
        start = start + bit * half

    def place(k, s):
        device, keep, give = table[s]
        half = chunk_units >> (s + 1)
        base = k * chunk_units
        return device, base + keep, base + give, half, base + chunk_units - 2 * half

    def swap(k, s):
        if s == 0:
            source = part.at[pl.ds(place(k, halves - 1)[1], kept_units)]
        else:
            source = swap_out.at[k, s - 1]
        return pltpu.make_async_remote_copy(
            src_ref=source,
            dst_ref=swap_in.at[k, s],
            send_sem=send_sem.at[k, halves + s],
            recv_sem=recv_sem.at[k, halves + s],
            device_id=pick(*swapping[s])[0],
            device_id_type=MESH,
        )

    def scatter(k, s):
        device, _, give, half, slot = place(k, s)
        return pltpu.make_async_remote_copy(
            src_ref=part.at[pl.ds(give, half)],
            dst_ref=landed.at[pl.ds(slot, half)],
            send_sem=send_sem.at[k, s],
            recv_sem=recv_sem.at[k, s],
            device_id=device,
            device_id_type=MESH,
        )

    def gather(k, s):
        device, keep, _, half, _ = place(k, s)
        return pltpu.make_async_remote_copy(
            src_ref=total.at[pl.ds(keep, half)],
            dst_ref=total.at[pl.ds(keep, half)],
            send_sem=send_sem.at[k, 2 * halves + swaps - 1 - s],
            recv_sem=recv_sem.at[k, 2 * halves + swaps - 1 - s],
            device_id=device,
            device_id_type=MESH,
        )

    def exchange_gram(s):
        device, _ = pick(*gram_order[s])
        return pltpu.make_async_remote_copy(
            src_ref=grams.at[s],
            dst_ref=gram_in.at[s],
            send_sem=gram_send.at[s],
            recv_sem=gram_recv.at[s],
            device_id=device,
            device_id_type=MESH,
        )

    def deliver(k):
        return pltpu.make_async_copy(
            staged.at[k, pl.ds(0, LANES)],
            projection_out.at[:, pl.ds(pl.multiple_of(k * chunk_cols, chunk_cols), chunk_cols)],
            out_sem.at[k],
        )

    def apply(k):
        inverse = work[:, LANES:]
        i_high, i_low = split(inverse)
        doubled = jnp.concatenate([i_high, i_high], axis=1)
        for i in range(strips):
            first = k * chunk_units + i * (STRIP // LANES) * per
            value = jnp.concatenate(
                [
                    total[pl.ds(first + j * per, per)].reshape(LANES, LANES)
                    for j in range(STRIP // LANES)
                ],
                axis=1,
            )
            v_high, v_low = split(value)
            staged[k, :LANES, i * STRIP : (i + 1) * STRIP] = jnp.dot(
                doubled, jnp.concatenate([v_high, v_low], axis=0), preferred_element_type=F32
            ) + jnp.dot(i_low, v_high, preferred_element_type=F32)
        deliver(k).start()

    last = 2 * halves + swaps

    def chunk_step(k, s):
        if s == 0:
            product(k)
            scatter(k, 0).start()
        elif s <= halves:
            scatter(k, s - 1).wait_recv()
            _, keep, _, half, slot = place(k, s - 1)
            part[pl.ds(keep, half)] = part[pl.ds(keep, half)] + landed[pl.ds(slot, half)]
            if s < halves:
                scatter(k, s).start()
            else:
                swap(k, 0).start()
        elif s <= halves + swaps:
            i = s - halves - 1
            swap(k, i).wait_recv()
            keep = place(k, halves - 1)[1]
            mine = part[pl.ds(keep, kept_units)] if i == 0 else swap_out[k, i - 1]
            value = mine + swap_in[k, i]
            if i + 1 < swaps:
                swap_out[k, i] = value
                swap(k, i + 1).start()
            else:
                total[pl.ds(keep, kept_units)] = value
                gather(k, halves - 1).start()
        else:
            gather(k, last - s).wait_recv()
            if s < last:
                gather(k, last - s - 1).start()
            else:
                apply(k)

    square_rows = lax.broadcasted_iota(jnp.int32, (LANES, LANES), 0)
    square_lanes = lax.broadcasted_iota(jnp.int32, (LANES, LANES), 1)
    panel_rows = lax.broadcasted_iota(jnp.int32, (PANEL, LANES), 0)
    panel_lanes = lax.broadcasted_iota(jnp.int32, (PANEL, LANES), 1)
    highest = lax.Precision.HIGHEST
    basis_copy = pltpu.make_async_copy(basis, basis_out, basis_sem)

    def gram_step(step):
        if step >= 1:
            exchange_gram(step - 1).wait_recv()
            grams[step] = grams[step - 1] + gram_in[step - 1]
        if step < bits:
            exchange_gram(step).start()
        else:
            work[:, :LANES] = grams[bits]
            work[:, LANES:] = (square_rows == square_lanes).astype(F32)

    def eliminate(base, piece):
        here = pl.ds(pl.multiple_of(base, PANEL), PANEL)
        if piece == 0:
            block = pltpu.roll(work[here, :LANES], (LANES - base) % LANES, 1)
            unit = (panel_rows + PANEL == panel_lanes).astype(F32)
            value = jnp.where(panel_lanes < PANEL, block, unit)
        else:
            value = panel[...]
        for j in range(piece * CHOL, (piece + 1) * CHOL, 2):
            first = jnp.broadcast_to(value[:, j : j + 1], (PANEL, LANES))
            second = jnp.broadcast_to(value[:, j + 1 : j + 2], (PANEL, LANES))
            ratio = first[j + 1 : j + 2, :] / first[j : j + 1, :]
            top = value[j : j + 1, :]
            next_row = value[j + 1 : j + 2, :] - ratio * top
            pivot = second[j + 1 : j + 2, :] - ratio * first[j + 1 : j + 2, :]
            change = first * (top / first[j : j + 1, :]) + (second - first * ratio) * (
                next_row / pivot
            )
            value = jnp.where(panel_rows > j + 1, value - change, value)
            value = jnp.where(panel_rows == j + 1, next_row, value)
        panel[...] = value
        if (piece + 1) * CHOL < PANEL:
            return
        diagonal = jnp.sum(
            jnp.where(panel_rows == panel_lanes, value, 0.0), axis=1, keepdims=True
        )
        value = pltpu.roll(value / jnp.sqrt(diagonal), (base + LANES - PANEL) % LANES, 1)
        inside = jnp.logical_and(panel_lanes >= base, panel_lanes < base + PANEL)
        value = jnp.where(inside, value, 0.0)
        done = jnp.dot(value, work[...], precision=highest, preferred_element_type=F32)
        work[here, :] = done
        change = jnp.dot(done[:, :LANES].T, done, precision=highest, preferred_element_type=F32)
        rest = lax.broadcasted_iota(jnp.int32, (LANES, 2 * LANES), 0) >= base + PANEL
        work[...] = jnp.where(rest, work[...] - change, work[...])

    def make_basis():
        product_turned = lax.dot_general(
            basis[...], work[:, LANES:], (((1,), (1,)), ((), ())),
            precision=highest, preferred_element_type=F32,
        )
        basis[...] = product_turned * math.sqrt(height * rows * cols)
        basis_copy.start()

    first_elimination = bits + 1
    pieces = PANEL // CHOL

    def tick(t, carry):
        for step in range(bits + 1):
            pl.when(t == step)(functools.partial(gram_step, step))
        for s in reversed(range(last + 1)):
            k = t - HOP * s
            pl.when(jnp.logical_and(k >= 0, k < chunks))(functools.partial(chunk_step, k, s))
        done = t - first_elimination
        for piece in range(pieces):
            due = jnp.logical_and(done >= 0, done < LANES // CHOL)
            base = done // pieces * PANEL
            pl.when(jnp.logical_and(due, done % pieces == piece))(
                functools.partial(eliminate, base, piece)
            )
        pl.when(done == LANES // CHOL)(make_basis)
        return carry

    lax.fori_loop(0, chunks + HOP * last, tick, 0)

    def drain(k, carry):
        for s in range(halves):
            scatter(k, s).wait_send()
            gather(k, s).wait_send()
        for s in range(swaps):
            swap(k, s).wait_send()
        deliver(k).wait()
        return carry

    lax.fori_loop(0, chunks, drain, 0)
    basis_copy.wait()
    for s in range(bits):
        exchange_gram(s).wait_send()


def hand_over(basis, projection, basis_out, projection_out, sems):
    copies = [pltpu.make_async_copy(basis, basis_out, sems.at[projection.shape[0] // TILE])]
    for i in range(projection.shape[0] // TILE):
        band = pl.ds(i * TILE, TILE)
        copies.append(
            pltpu.make_async_copy(projection.at[band], projection_out.at[band], sems.at[i])
        )
    for copy in copies:
        copy.start()
    for copy in copies:
        copy.wait()


def per_device(rows, cols, slab, sketch):
    height, width = slab.shape
    rank = sketch.shape[1]
    bits = (rows * cols).bit_length() - 1
    units = width // LANES * (rank // TILE)
    halves, swaps = (len(part) for part in orders(rows, cols))
    kept = (units // CHUNKS) >> halves
    anywhere = pl.BlockSpec(memory_space=pl.ANY)
    basis, projection = pl.pallas_call(
        functools.partial(sum_kernel, rows, cols),
        out_shape=(
            jax.ShapeDtypeStruct((height, rank), F32),
            jax.ShapeDtypeStruct((rank, width), F32),
        ),
        in_specs=[anywhere] * 2,
        out_specs=(anywhere,) * 2,
        scratch_shapes=[
            pltpu.VMEM((width // LOAD, height, LOAD), F32),
            pltpu.VMEM((width, rank), F32),
            pltpu.VMEM((height, width), BF16),
            pltpu.VMEM((height, width), BF16),
            pltpu.VMEM((units, TILE, LANES), F32),
            pltpu.VMEM((units, TILE, LANES), F32),
            pltpu.VMEM((units, TILE, LANES), F32),
            pltpu.VMEM((CHUNKS, swaps, kept, TILE, LANES), F32),
            pltpu.VMEM((CHUNKS, swaps, kept, TILE, LANES), F32),
            pltpu.VMEM((height, rank), F32),
            pltpu.VMEM((2 * rank, height), BF16),
            pltpu.VMEM((bits + 1, rank, rank), F32),
            pltpu.VMEM((bits, rank, rank), F32),
            pltpu.VMEM((rank, 2 * rank), F32),
            pltpu.VMEM((PANEL, rank), F32),
            pltpu.VMEM((height, 2 * rank), F32),
            pltpu.SemaphoreType.DMA((width // LOAD,)),
            pltpu.SemaphoreType.DMA,
            pltpu.SemaphoreType.DMA((CHUNKS, 2 * halves + swaps)),
            pltpu.SemaphoreType.DMA((CHUNKS, 2 * halves + swaps)),
            pltpu.SemaphoreType.DMA((bits,)),
            pltpu.SemaphoreType.DMA((bits,)),
            pltpu.SemaphoreType.DMA((CHUNKS,)),
            pltpu.SemaphoreType.DMA,
        ],
        compiler_params=pltpu.CompilerParams(
            collective_id=0, has_side_effects=True, vmem_limit_bytes=56 * 2**20
        ),
    )(slab, sketch)
    return pl.pallas_call(
        hand_over,
        out_shape=(
            jax.ShapeDtypeStruct((height, rank), F32),
            jax.ShapeDtypeStruct((rank, width), F32),
        ),
        in_specs=[anywhere] * 2,
        out_specs=(anywhere,) * 2,
        scratch_shapes=[pltpu.SemaphoreType.DMA((rank // TILE + 1,))],
        compiler_params=pltpu.CompilerParams(vmem_limit_bytes=56 * 2**20),
    )(basis, projection)


def solution(mesh):
    rows, cols = mesh.shape["row"], mesh.shape["col"]
    placed = (P(("row", "col"), None), P())
    return jax.shard_map(
        functools.partial(per_device, rows, cols),
        mesh=mesh,
        in_specs=placed,
        out_specs=placed,
        check_vma=False,
    )
```

```python
import functools
import math

import jax
import jax.numpy as jnp
from jax import lax
from jax.experimental import pallas as pl
from jax.experimental.pallas import tpu as pltpu
from jax.sharding import PartitionSpec as P

MESH = pl.DeviceIdType.MESH
BF16 = jnp.bfloat16
F32 = jnp.float32
LANES = 128
TILE = 8
LOAD = 1024
CHUNKS = 8
STRIP = 512
HOP = 2
PANEL = 32
CHOL = 16


def split(value):
    high = value.astype(BF16)
    return high, (value - high.astype(F32)).astype(BF16)


def bit_of(axis, bit):
    index = lax.axis_index(axis)
    value = (index // 2**bit) % 2
    return {axis: 2**bit * (1 - 2 * value)}, value


def orders(rows, cols):
    row_bits = [("row", b) for b in range(1, rows.bit_length() - 1)]
    col_bits = [("col", b) for b in range(cols.bit_length() - 1)]
    inner = 1 if len(col_bits) == 3 else len(col_bits) // 2
    near, far = col_bits[:inner], col_bits[inner:]
    core = [("row", 0)]
    even, odd = core + near + far[:1] + row_bits, core + row_bits + far[:1] + near
    return list(zip(even, odd)), [(b, b) for b in far[1:]]


def pick(even, odd):
    core = lax.axis_index("row") % 2
    device = {"row": lax.axis_index("row"), "col": lax.axis_index("col")}
    bit = 0
    for (axis, place), weight in ((even, 1 - core), (odd, core)):
        step, value = bit_of(axis, place)
        device[axis] = device[axis] + weight * step[axis]
        bit = bit + weight * value
    return (device["row"], device["col"]), bit


def sum_kernel(
    rows, cols, slab, sketch, basis_out, projection_out,
    staged, sk, high, low, part, landed, total, swap_in, swap_out, basis, left, grams, gram_in, work, panel, wide_acc,
    slab_sem, sk_sem, send_sem, recv_sem, gram_send, gram_recv, out_sem, basis_sem,
):
    height, width = slab.shape
    bits = (rows * cols).bit_length() - 1
    units = width // LANES * (LANES // TILE)
    chunks = CHUNKS
    chunk_units = units // chunks
    chunk_cols = width // chunks
    loads = width // LOAD

    sketch_copy = pltpu.make_async_copy(sketch, sk, sk_sem)
    sketch_copy.start()

    def load(i):
        return pltpu.make_async_copy(
            slab.at[:, pl.ds(pl.multiple_of(i * LOAD, LOAD), LOAD)], staged.at[i], slab_sem.at[i]
        )

    for i in range(loads):
        load(i).start()

    halving, swapping = orders(rows, cols)
    halves, swaps = len(halving), len(swapping)
    kept_units = chunk_units >> halves
    gram_order = [(even, even) for even, _ in halving + swapping]
    barrier = pltpu.get_barrier_semaphore()
    for place in gram_order:
        device, _ = pick(*place)
        pl.semaphore_signal(barrier, inc=1, device_id=device, device_id_type=MESH)

    wide_acc[...] = jnp.zeros_like(wide_acc)
    sketch_copy.wait()

    def sample(i, carry):
        load(i).wait()
        a_high, a_low = split(staged[i])
        columns = pl.ds(pl.multiple_of(i * LOAD, LOAD), LOAD)
        high[:, columns] = a_high
        low[:, columns] = a_low
        s_high, s_low = split(sk[columns, :])
        both = jnp.concatenate([s_high, s_low], axis=1)
        wide_acc[...] += jnp.dot(a_high, both, preferred_element_type=F32)
        wide_acc[:, :LANES] += jnp.dot(a_low, s_high, preferred_element_type=F32)
        return carry

    lax.fori_loop(0, loads, sample, 0)
    sampled = wide_acc[:, :LANES] + wide_acc[:, LANES:]
    basis[...] = sampled
    turned = sampled.T
    t_high, t_low = split(turned)
    left[:LANES, :] = t_high
    left[LANES:, :] = t_low
    grams[0] = jnp.dot(
        turned, sampled, precision=lax.Precision.HIGHEST, preferred_element_type=F32
    )
    pl.semaphore_wait(barrier, bits)

    per = LANES // TILE
    strips = chunk_cols // STRIP

    def product(k):
        for i in range(strips):
            columns = pl.ds(pl.multiple_of((k * strips + i) * STRIP, STRIP), STRIP)
            both = jnp.dot(left[...], high[:, columns], preferred_element_type=F32)
            more = jnp.dot(left[:LANES, :], low[:, columns], preferred_element_type=F32)
            value = both[:LANES] + both[LANES:] + more
            for j in range(STRIP // LANES):
                first = k * chunk_units + (i * (STRIP // LANES) + j) * per
                part[pl.ds(first, per)] = value[:, j * LANES : (j + 1) * LANES].reshape(
                    per, TILE, LANES
                )

    table, start = [], 0
    for s, places in enumerate(halving):
        device, bit = pick(*places)
        half = chunk_units >> (s + 1)
        table.append((device, start + bit * half, start + (1 - bit) * half))
        start = start + bit * half

    def place(k, s):
        device, keep, give = table[s]
        half = chunk_units >> (s + 1)
        base = k * chunk_units
        return device, base + keep, base + give, half, base + chunk_units - 2 * half

    def swap(k, s):
        if s == 0:
            source = part.at[pl.ds(place(k, halves - 1)[1], kept_units)]
        else:
            source = swap_out.at[k, s - 1]
        return pltpu.make_async_remote_copy(
            src_ref=source,
            dst_ref=swap_in.at[k, s],
            send_sem=send_sem.at[k, halves + s],
            recv_sem=recv_sem.at[k, halves + s],
            device_id=pick(*swapping[s])[0],
            device_id_type=MESH,
        )

    def scatter(k, s):
        device, _, give, half, slot = place(k, s)
        return pltpu.make_async_remote_copy(
            src_ref=part.at[pl.ds(give, half)],
            dst_ref=landed.at[pl.ds(slot, half)],
            send_sem=send_sem.at[k, s],
            recv_sem=recv_sem.at[k, s],
            device_id=device,
            device_id_type=MESH,
        )

    def gather(k, s):
        device, keep, _, half, _ = place(k, s)
        return pltpu.make_async_remote_copy(
            src_ref=total.at[pl.ds(keep, half)],
            dst_ref=total.at[pl.ds(keep, half)],
            send_sem=send_sem.at[k, 2 * halves + swaps - 1 - s],
            recv_sem=recv_sem.at[k, 2 * halves + swaps - 1 - s],
            device_id=device,
            device_id_type=MESH,
        )

    def exchange_gram(s):
        device, _ = pick(*gram_order[s])
        return pltpu.make_async_remote_copy(
            src_ref=grams.at[s],
            dst_ref=gram_in.at[s],
            send_sem=gram_send.at[s],
            recv_sem=gram_recv.at[s],
            device_id=device,
            device_id_type=MESH,
        )

    def deliver(k):
        return pltpu.make_async_copy(
            staged.at[k, pl.ds(0, LANES)],
            projection_out.at[:, pl.ds(pl.multiple_of(k * chunk_cols, chunk_cols), chunk_cols)],
            out_sem.at[k],
        )

    def apply(k):
        inverse = work[:, LANES:]
        i_high, i_low = split(inverse)
        doubled = jnp.concatenate([i_high, i_high], axis=1)
        for i in range(strips):
            first = k * chunk_units + i * (STRIP // LANES) * per
            value = jnp.concatenate(
                [
                    total[pl.ds(first + j * per, per)].reshape(LANES, LANES)
                    for j in range(STRIP // LANES)
                ],
                axis=1,
            )
            v_high, v_low = split(value)
            staged[k, :LANES, i * STRIP : (i + 1) * STRIP] = jnp.dot(
                doubled, jnp.concatenate([v_high, v_low], axis=0), preferred_element_type=F32
            ) + jnp.dot(i_low, v_high, preferred_element_type=F32)
        deliver(k).start()

    last = 2 * halves + swaps

    def chunk_step(k, s):
        if s == 0:
            product(k)
            scatter(k, 0).start()
        elif s <= halves:
            scatter(k, s - 1).wait_recv()
            _, keep, _, half, slot = place(k, s - 1)
            part[pl.ds(keep, half)] = part[pl.ds(keep, half)] + landed[pl.ds(slot, half)]
            if s < halves:
                scatter(k, s).start()
            else:
                swap(k, 0).start()
        elif s <= halves + swaps:
            i = s - halves - 1
            swap(k, i).wait_recv()
            keep = place(k, halves - 1)[1]
            mine = part[pl.ds(keep, kept_units)] if i == 0 else swap_out[k, i - 1]
            value = mine + swap_in[k, i]
            if i + 1 < swaps:
                swap_out[k, i] = value
                swap(k, i + 1).start()
            else:
                total[pl.ds(keep, kept_units)] = value
                gather(k, halves - 1).start()
        else:
            gather(k, last - s).wait_recv()
            if s < last:
                gather(k, last - s - 1).start()
            else:
                apply(k)

    square_rows = lax.broadcasted_iota(jnp.int32, (LANES, LANES), 0)
    square_lanes = lax.broadcasted_iota(jnp.int32, (LANES, LANES), 1)
    panel_rows = lax.broadcasted_iota(jnp.int32, (PANEL, LANES), 0)
    panel_lanes = lax.broadcasted_iota(jnp.int32, (PANEL, LANES), 1)
    highest = lax.Precision.HIGHEST
    basis_copy = pltpu.make_async_copy(basis, basis_out, basis_sem)

    def gram_step(step):
        if step >= 1:
            exchange_gram(step - 1).wait_recv()
            grams[step] = grams[step - 1] + gram_in[step - 1]
        if step < bits:
            exchange_gram(step).start()
        else:
            work[:, :LANES] = grams[bits]
            work[:, LANES:] = (square_rows == square_lanes).astype(F32)

    def eliminate(base, piece):
        here = pl.ds(pl.multiple_of(base, PANEL), PANEL)
        if piece == 0:
            block = pltpu.roll(work[here, :LANES], (LANES - base) % LANES, 1)
            unit = (panel_rows + PANEL == panel_lanes).astype(F32)
            value = jnp.where(panel_lanes < PANEL, block, unit)
        else:
            value = panel[...]
        for j in range(piece * CHOL, (piece + 1) * CHOL, 2):
            first = jnp.broadcast_to(value[:, j : j + 1], (PANEL, LANES))
            second = jnp.broadcast_to(value[:, j + 1 : j + 2], (PANEL, LANES))
            ratio = first[j + 1 : j + 2, :] / first[j : j + 1, :]
            top = value[j : j + 1, :]
            next_row = value[j + 1 : j + 2, :] - ratio * top
            pivot = second[j + 1 : j + 2, :] - ratio * first[j + 1 : j + 2, :]
            change = first * (top / first[j : j + 1, :]) + (second - first * ratio) * (
                next_row / pivot
            )
            value = jnp.where(panel_rows > j + 1, value - change, value)
            value = jnp.where(panel_rows == j + 1, next_row, value)
        panel[...] = value
        if (piece + 1) * CHOL < PANEL:
            return
        diagonal = jnp.sum(
            jnp.where(panel_rows == panel_lanes, value, 0.0), axis=1, keepdims=True
        )
        value = pltpu.roll(value / jnp.sqrt(diagonal), (base + LANES - PANEL) % LANES, 1)
        inside = jnp.logical_and(panel_lanes >= base, panel_lanes < base + PANEL)
        value = jnp.where(inside, value, 0.0)
        done = jnp.dot(value, work[...], precision=highest, preferred_element_type=F32)
        work[here, :] = done
        change = jnp.dot(done[:, :LANES].T, done, precision=highest, preferred_element_type=F32)
        rest = lax.broadcasted_iota(jnp.int32, (LANES, 2 * LANES), 0) >= base + PANEL
        work[...] = jnp.where(rest, work[...] - change, work[...])

    def make_basis():
        product_turned = lax.dot_general(
            basis[...], work[:, LANES:], (((1,), (1,)), ((), ())),
            precision=highest, preferred_element_type=F32,
        )
        basis[...] = product_turned * math.sqrt(height * rows * cols)
        basis_copy.start()

    first_elimination = bits + 1
    pieces = PANEL // CHOL

    def tick(t, carry):
        for step in range(bits + 1):
            pl.when(t == step)(functools.partial(gram_step, step))
        for s in reversed(range(last + 1)):
            k = t - HOP * s
            pl.when(jnp.logical_and(k >= 0, k < chunks))(functools.partial(chunk_step, k, s))
        done = t - first_elimination
        for piece in range(pieces):
            due = jnp.logical_and(done >= 0, done < LANES // CHOL)
            base = done // pieces * PANEL
            pl.when(jnp.logical_and(due, done % pieces == piece))(
                functools.partial(eliminate, base, piece)
            )
        pl.when(done == LANES // CHOL)(make_basis)
        return carry

    lax.fori_loop(0, chunks + HOP * last, tick, 0)

    def drain(k, carry):
        for s in range(halves):
            scatter(k, s).wait_send()
            gather(k, s).wait_send()
        for s in range(swaps):
            swap(k, s).wait_send()
        deliver(k).wait()
        return carry

    lax.fori_loop(0, chunks, drain, 0)
    basis_copy.wait()
    for s in range(bits):
        exchange_gram(s).wait_send()


def hand_over(basis, projection, basis_out, projection_out, basis_held, held, reads, writes):
    pieces, height, _ = held.shape
    moves = [(basis, basis_held, basis_out)]
    for i in range(pieces):
        band = pl.ds(i * height, height)
        moves.append((projection.at[band], held.at[i], projection_out.at[band]))
    for i, (source, middle, _) in enumerate(moves):
        pltpu.make_async_copy(source, middle, reads.at[i]).start()
    for i, (source, middle, target) in enumerate(moves):
        pltpu.make_async_copy(source, middle, reads.at[i]).wait()
        pltpu.make_async_copy(middle, target, writes.at[i]).start()
    for i, (_, middle, target) in enumerate(moves):
        pltpu.make_async_copy(middle, target, writes.at[i]).wait()


def per_device(rows, cols, slab, sketch):
    height, width = slab.shape
    rank = sketch.shape[1]
    bits = (rows * cols).bit_length() - 1
    units = width // LANES * (rank // TILE)
    halves, swaps = (len(part) for part in orders(rows, cols))
    kept = (units // CHUNKS) >> halves
    anywhere = pl.BlockSpec(memory_space=pl.ANY)
    basis, projection = pl.pallas_call(
        functools.partial(sum_kernel, rows, cols),
        out_shape=(
            jax.ShapeDtypeStruct((height, rank), F32),
            jax.ShapeDtypeStruct((rank, width), F32),
        ),
        in_specs=[anywhere] * 2,
        out_specs=(anywhere,) * 2,
        scratch_shapes=[
            pltpu.VMEM((width // LOAD, height, LOAD), F32),
            pltpu.VMEM((width, rank), F32),
            pltpu.VMEM((height, width), BF16),
            pltpu.VMEM((height, width), BF16),
            pltpu.VMEM((units, TILE, LANES), F32),
            pltpu.VMEM((units, TILE, LANES), F32),
            pltpu.VMEM((units, TILE, LANES), F32),
            pltpu.VMEM((CHUNKS, swaps, kept, TILE, LANES), F32),
            pltpu.VMEM((CHUNKS, swaps, kept, TILE, LANES), F32),
            pltpu.VMEM((height, rank), F32),
            pltpu.VMEM((2 * rank, height), BF16),
            pltpu.VMEM((bits + 1, rank, rank), F32),
            pltpu.VMEM((bits, rank, rank), F32),
            pltpu.VMEM((rank, 2 * rank), F32),
            pltpu.VMEM((PANEL, rank), F32),
            pltpu.VMEM((height, 2 * rank), F32),
            pltpu.SemaphoreType.DMA((width // LOAD,)),
            pltpu.SemaphoreType.DMA,
            pltpu.SemaphoreType.DMA((CHUNKS, 2 * halves + swaps)),
            pltpu.SemaphoreType.DMA((CHUNKS, 2 * halves + swaps)),
            pltpu.SemaphoreType.DMA((bits,)),
            pltpu.SemaphoreType.DMA((bits,)),
            pltpu.SemaphoreType.DMA((CHUNKS,)),
            pltpu.SemaphoreType.DMA,
        ],
        compiler_params=pltpu.CompilerParams(
            collective_id=0, has_side_effects=True, vmem_limit_bytes=56 * 2**20
        ),
    )(slab, sketch)
    return pl.pallas_call(
        hand_over,
        out_shape=(
            jax.ShapeDtypeStruct((height, rank), F32),
            jax.ShapeDtypeStruct((rank, width), F32),
        ),
        in_specs=[anywhere] * 2,
        out_specs=(anywhere,) * 2,
        scratch_shapes=[
            pltpu.VMEM((height, rank), F32),
            pltpu.VMEM((rank // TILE, TILE, width), F32),
            pltpu.SemaphoreType.DMA((rank // TILE + 1,)),
            pltpu.SemaphoreType.DMA((rank // TILE + 1,)),
        ],
        compiler_params=pltpu.CompilerParams(vmem_limit_bytes=56 * 2**20),
    )(basis, projection)


def solution(mesh):
    rows, cols = mesh.shape["row"], mesh.shape["col"]
    placed = (P(("row", "col"), None), P())
    return jax.shard_map(
        functools.partial(per_device, rows, cols),
        mesh=mesh,
        in_specs=placed,
        out_specs=placed,
        check_vma=False,
    )
```

```python
import functools
import math

import jax
import jax.numpy as jnp
from jax import lax
from jax.experimental import pallas as pl
from jax.experimental.pallas import tpu as pltpu
from jax.sharding import PartitionSpec as P

MESH = pl.DeviceIdType.MESH
BF16 = jnp.bfloat16
F32 = jnp.float32
LANES = 128
TILE = 8
LOAD = 1024
CHUNKS = 8
STRIP = 512
SPACING = 2
GRAM_HOP = 2
PANEL = 32
CHOL = 8


def split(value):
    high = value.astype(BF16)
    return high, (value - high.astype(F32)).astype(BF16)


def bit_of(axis, bit):
    index = lax.axis_index(axis)
    value = (index // 2**bit) % 2
    return {axis: 2**bit * (1 - 2 * value)}, value


def orders(rows, cols):
    row_bits = [("row", b) for b in range(1, rows.bit_length() - 1)]
    col_bits = [("col", b) for b in range(cols.bit_length() - 1)]
    inner = 1 if len(col_bits) == 3 else len(col_bits) // 2
    near, far = col_bits[:inner], col_bits[inner:]
    core = [("row", 0)]
    even, odd = core + near + far[:1] + row_bits, core + row_bits + far[:1] + near
    return list(zip(even, odd)), [(b, b) for b in far[1:]]


def pick(even, odd):
    core = lax.axis_index("row") % 2
    device = {"row": lax.axis_index("row"), "col": lax.axis_index("col")}
    bit = 0
    for (axis, place), weight in ((even, 1 - core), (odd, core)):
        step, value = bit_of(axis, place)
        device[axis] = device[axis] + weight * step[axis]
        bit = bit + weight * value
    return (device["row"], device["col"]), bit


def sum_kernel(
    rows, cols, slab, sketch, basis_out, projection_out,
    staged, sk, high, low, part, landed, total, swap_in, swap_out, basis, left, grams, gram_in, work, panel, wide_acc,
    slab_sem, sk_sem, send_sem, recv_sem, gram_send, gram_recv, out_sem, basis_sem,
):
    height, width = slab.shape
    bits = (rows * cols).bit_length() - 1
    units = width // LANES * (LANES // TILE)
    chunks = CHUNKS
    chunk_units = units // chunks
    chunk_cols = width // chunks
    loads = width // LOAD

    sketch_copy = pltpu.make_async_copy(sketch, sk, sk_sem)
    sketch_copy.start()

    def load(i):
        return pltpu.make_async_copy(
            slab.at[:, pl.ds(pl.multiple_of(i * LOAD, LOAD), LOAD)], staged.at[i], slab_sem.at[i]
        )

    for i in range(loads):
        load(i).start()

    halving, swapping = orders(rows, cols)
    halves, swaps = len(halving), len(swapping)
    kept_units = chunk_units >> halves
    gram_order = [(even, even) for even, _ in halving + swapping]
    barrier = pltpu.get_barrier_semaphore()
    for place in gram_order:
        device, _ = pick(*place)
        pl.semaphore_signal(barrier, inc=1, device_id=device, device_id_type=MESH)

    wide_acc[...] = jnp.zeros_like(wide_acc)
    sketch_copy.wait()

    def sample(i, carry):
        load(i).wait()
        a_high, a_low = split(staged[i])
        columns = pl.ds(pl.multiple_of(i * LOAD, LOAD), LOAD)
        high[:, columns] = a_high
        low[:, columns] = a_low
        s_high, s_low = split(sk[columns, :])
        both = jnp.concatenate([s_high, s_low], axis=1)
        wide_acc[...] += jnp.dot(a_high, both, preferred_element_type=F32)
        wide_acc[:, :LANES] += jnp.dot(a_low, s_high, preferred_element_type=F32)
        return carry

    lax.fori_loop(0, loads, sample, 0)
    sampled = wide_acc[:, :LANES] + wide_acc[:, LANES:]
    basis[...] = sampled
    turned = sampled.T
    t_high, t_low = split(turned)
    left[:LANES, :] = t_high
    left[LANES:, :] = t_low
    grams[0] = jnp.dot(
        turned, sampled, precision=lax.Precision.HIGHEST, preferred_element_type=F32
    )
    pl.semaphore_wait(barrier, bits)

    per = LANES // TILE
    strips = chunk_cols // STRIP

    def product(k):
        for i in range(strips):
            columns = pl.ds(pl.multiple_of((k * strips + i) * STRIP, STRIP), STRIP)
            both = jnp.dot(left[...], high[:, columns], preferred_element_type=F32)
            more = jnp.dot(left[:LANES, :], low[:, columns], preferred_element_type=F32)
            value = both[:LANES] + both[LANES:] + more
            for j in range(STRIP // LANES):
                first = k * chunk_units + (i * (STRIP // LANES) + j) * per
                part[pl.ds(first, per)] = value[:, j * LANES : (j + 1) * LANES].reshape(
                    per, TILE, LANES
                )

    table, start = [], 0
    for s, places in enumerate(halving):
        device, bit = pick(*places)
        half = chunk_units >> (s + 1)
        table.append((device, start + bit * half, start + (1 - bit) * half))
        start = start + bit * half

    def place(k, s):
        device, keep, give = table[s]
        half = chunk_units >> (s + 1)
        base = k * chunk_units
        return device, base + keep, base + give, half, base + chunk_units - 2 * half

    def swap(k, s):
        if s == 0:
            source = part.at[pl.ds(place(k, halves - 1)[1], kept_units)]
        else:
            source = swap_out.at[k, s - 1]
        return pltpu.make_async_remote_copy(
            src_ref=source,
            dst_ref=swap_in.at[k, s],
            send_sem=send_sem.at[k, halves + s],
            recv_sem=recv_sem.at[k, halves + s],
            device_id=pick(*swapping[s])[0],
            device_id_type=MESH,
        )

    def scatter(k, s):
        device, _, give, half, slot = place(k, s)
        return pltpu.make_async_remote_copy(
            src_ref=part.at[pl.ds(give, half)],
            dst_ref=landed.at[pl.ds(slot, half)],
            send_sem=send_sem.at[k, s],
            recv_sem=recv_sem.at[k, s],
            device_id=device,
            device_id_type=MESH,
        )

    def gather(k, s):
        device, keep, _, half, _ = place(k, s)
        return pltpu.make_async_remote_copy(
            src_ref=total.at[pl.ds(keep, half)],
            dst_ref=total.at[pl.ds(keep, half)],
            send_sem=send_sem.at[k, 2 * halves + swaps - 1 - s],
            recv_sem=recv_sem.at[k, 2 * halves + swaps - 1 - s],
            device_id=device,
            device_id_type=MESH,
        )

    def exchange_gram(s):
        device, _ = pick(*gram_order[s])
        return pltpu.make_async_remote_copy(
            src_ref=grams.at[s],
            dst_ref=gram_in.at[s],
            send_sem=gram_send.at[s],
            recv_sem=gram_recv.at[s],
            device_id=device,
            device_id_type=MESH,
        )

    def deliver(k):
        return pltpu.make_async_copy(
            staged.at[k, pl.ds(0, LANES)],
            projection_out.at[:, pl.ds(pl.multiple_of(k * chunk_cols, chunk_cols), chunk_cols)],
            out_sem.at[k],
        )

    def apply(k):
        inverse = work[:, LANES:]
        i_high, i_low = split(inverse)
        doubled = jnp.concatenate([i_high, i_high], axis=1)
        for i in range(strips):
            first = k * chunk_units + i * (STRIP // LANES) * per
            value = jnp.concatenate(
                [
                    total[pl.ds(first + j * per, per)].reshape(LANES, LANES)
                    for j in range(STRIP // LANES)
                ],
                axis=1,
            )
            v_high, v_low = split(value)
            staged[k, :LANES, i * STRIP : (i + 1) * STRIP] = jnp.dot(
                doubled, jnp.concatenate([v_high, v_low], axis=0), preferred_element_type=F32
            ) + jnp.dot(i_low, v_high, preferred_element_type=F32)
        deliver(k).start()

    last = 2 * halves + swaps

    def chunk_step(k, s):
        if s == 0:
            product(k)
            scatter(k, 0).start()
        elif s <= halves:
            scatter(k, s - 1).wait_recv()
            _, keep, _, half, slot = place(k, s - 1)
            part[pl.ds(keep, half)] = part[pl.ds(keep, half)] + landed[pl.ds(slot, half)]
            if s < halves:
                scatter(k, s).start()
            else:
                swap(k, 0).start()
        elif s <= halves + swaps:
            i = s - halves - 1
            swap(k, i).wait_recv()
            keep = place(k, halves - 1)[1]
            mine = part[pl.ds(keep, kept_units)] if i == 0 else swap_out[k, i - 1]
            value = mine + swap_in[k, i]
            if i + 1 < swaps:
                swap_out[k, i] = value
                swap(k, i + 1).start()
            else:
                total[pl.ds(keep, kept_units)] = value
                gather(k, halves - 1).start()
        else:
            gather(k, last - s).wait_recv()
            if s < last:
                gather(k, last - s - 1).start()

    square_rows = lax.broadcasted_iota(jnp.int32, (LANES, LANES), 0)
    square_lanes = lax.broadcasted_iota(jnp.int32, (LANES, LANES), 1)
    panel_rows = lax.broadcasted_iota(jnp.int32, (PANEL, LANES), 0)
    panel_lanes = lax.broadcasted_iota(jnp.int32, (PANEL, LANES), 1)
    highest = lax.Precision.HIGHEST
    basis_copy = pltpu.make_async_copy(basis, basis_out, basis_sem)

    def gram_step(step):
        if step >= 1:
            exchange_gram(step - 1).wait_recv()
            grams[step] = grams[step - 1] + gram_in[step - 1]
        if step < bits:
            exchange_gram(step).start()
        else:
            work[:, :LANES] = grams[bits]
            work[:, LANES:] = (square_rows == square_lanes).astype(F32)

    def eliminate(base, piece):
        here = pl.ds(pl.multiple_of(base, PANEL), PANEL)
        if piece == 0:
            block = pltpu.roll(work[here, :LANES], (LANES - base) % LANES, 1)
            unit = (panel_rows + PANEL == panel_lanes).astype(F32)
            value = jnp.where(panel_lanes < PANEL, block, unit)
        else:
            value = panel[...]
        for j in range(piece * CHOL, (piece + 1) * CHOL, 2):
            first = jnp.broadcast_to(value[:, j : j + 1], (PANEL, LANES))
            second = jnp.broadcast_to(value[:, j + 1 : j + 2], (PANEL, LANES))
            ratio = first[j + 1 : j + 2, :] / first[j : j + 1, :]
            top = value[j : j + 1, :]
            next_row = value[j + 1 : j + 2, :] - ratio * top
            pivot = second[j + 1 : j + 2, :] - ratio * first[j + 1 : j + 2, :]
            change = first * (top / first[j : j + 1, :]) + (second - first * ratio) * (
                next_row / pivot
            )
            value = jnp.where(panel_rows > j + 1, value - change, value)
            value = jnp.where(panel_rows == j + 1, next_row, value)
        panel[...] = value
        if (piece + 1) * CHOL < PANEL:
            return
        diagonal = jnp.sum(
            jnp.where(panel_rows == panel_lanes, value, 0.0), axis=1, keepdims=True
        )
        value = pltpu.roll(value / jnp.sqrt(diagonal), (base + LANES - PANEL) % LANES, 1)
        inside = jnp.logical_and(panel_lanes >= base, panel_lanes < base + PANEL)
        value = jnp.where(inside, value, 0.0)
        done = jnp.dot(value, work[...], precision=highest, preferred_element_type=F32)
        work[here, :] = done
        change = jnp.dot(done[:, :LANES].T, done, precision=highest, preferred_element_type=F32)
        rest = lax.broadcasted_iota(jnp.int32, (LANES, 2 * LANES), 0) >= base + PANEL
        work[...] = jnp.where(rest, work[...] - change, work[...])

    def make_basis():
        product_turned = lax.dot_general(
            basis[...], work[:, LANES:], (((1,), (1,)), ((), ())),
            precision=highest, preferred_element_type=F32,
        )
        basis[...] = product_turned * math.sqrt(height * rows * cols)
        basis_copy.start()

    first_elimination = GRAM_HOP * bits + 1
    eliminations = LANES // CHOL
    hops = [2 if s == 0 or s > 2 else 3 for s in range(halves)]
    due_at = [0]
    for hop in hops + [3] * swaps + hops[::-1]:
        due_at.append(due_at[-1] + hop)
    apply_at = [
        max(due_at[-1] + SPACING * k, first_elimination + eliminations + 1 + k)
        for k in range(chunks)
    ]
    pieces = PANEL // CHOL

    def tick(t, carry):
        for step in range(bits + 1):
            pl.when(t == GRAM_HOP * step)(functools.partial(gram_step, step))
        for s in reversed(range(last + 1)):
            since = t - due_at[s]
            due = jnp.logical_and(since >= 0, since < SPACING * chunks)
            due = jnp.logical_and(due, since % SPACING == 0)
            pl.when(due)(functools.partial(chunk_step, since // SPACING, s))
        done = t - first_elimination
        for piece in range(pieces):
            due = jnp.logical_and(done >= 0, done < eliminations)
            base = done // pieces * PANEL
            pl.when(jnp.logical_and(due, done % pieces == piece))(
                functools.partial(eliminate, base, piece)
            )
        pl.when(done == eliminations)(make_basis)
        ready, finished = 0, 0
        for k, time in enumerate(apply_at):
            now = jnp.where(t == time, 1, 0)
            ready, finished = ready + now, finished + now * k
        pl.when(ready > 0)(functools.partial(apply, finished))
        return carry

    lax.fori_loop(0, apply_at[-1] + 1, tick, 0)

    def drain(k, carry):
        for s in range(halves):
            scatter(k, s).wait_send()
            gather(k, s).wait_send()
        for s in range(swaps):
            swap(k, s).wait_send()
        deliver(k).wait()
        return carry

    lax.fori_loop(0, chunks, drain, 0)
    basis_copy.wait()
    for s in range(bits):
        exchange_gram(s).wait_send()


def hand_over(basis, projection, basis_out, projection_out, basis_held, held, reads, writes):
    pieces, height, _ = held.shape
    moves = [(basis, basis_held, basis_out)]
    for i in range(pieces):
        band = pl.ds(i * height, height)
        moves.append((projection.at[band], held.at[i], projection_out.at[band]))
    for i, (source, middle, _) in enumerate(moves):
        pltpu.make_async_copy(source, middle, reads.at[i]).start()
    for i, (source, middle, target) in enumerate(moves):
        pltpu.make_async_copy(source, middle, reads.at[i]).wait()
        pltpu.make_async_copy(middle, target, writes.at[i]).start()
    for i, (_, middle, target) in enumerate(moves):
        pltpu.make_async_copy(middle, target, writes.at[i]).wait()


def per_device(rows, cols, slab, sketch):
    height, width = slab.shape
    rank = sketch.shape[1]
    bits = (rows * cols).bit_length() - 1
    units = width // LANES * (rank // TILE)
    halves, swaps = (len(part) for part in orders(rows, cols))
    kept = (units // CHUNKS) >> halves
    anywhere = pl.BlockSpec(memory_space=pl.ANY)
    basis, projection = pl.pallas_call(
        functools.partial(sum_kernel, rows, cols),
        out_shape=(
            jax.ShapeDtypeStruct((height, rank), F32),
            jax.ShapeDtypeStruct((rank, width), F32),
        ),
        in_specs=[anywhere] * 2,
        out_specs=(anywhere,) * 2,
        scratch_shapes=[
            pltpu.VMEM((width // LOAD, height, LOAD), F32),
            pltpu.VMEM((width, rank), F32),
            pltpu.VMEM((height, width), BF16),
            pltpu.VMEM((height, width), BF16),
            pltpu.VMEM((units, TILE, LANES), F32),
            pltpu.VMEM((units, TILE, LANES), F32),
            pltpu.VMEM((units, TILE, LANES), F32),
            pltpu.VMEM((CHUNKS, swaps, kept, TILE, LANES), F32),
            pltpu.VMEM((CHUNKS, swaps, kept, TILE, LANES), F32),
            pltpu.VMEM((height, rank), F32),
            pltpu.VMEM((2 * rank, height), BF16),
            pltpu.VMEM((bits + 1, rank, rank), F32),
            pltpu.VMEM((bits, rank, rank), F32),
            pltpu.VMEM((rank, 2 * rank), F32),
            pltpu.VMEM((PANEL, rank), F32),
            pltpu.VMEM((height, 2 * rank), F32),
            pltpu.SemaphoreType.DMA((width // LOAD,)),
            pltpu.SemaphoreType.DMA,
            pltpu.SemaphoreType.DMA((CHUNKS, 2 * halves + swaps)),
            pltpu.SemaphoreType.DMA((CHUNKS, 2 * halves + swaps)),
            pltpu.SemaphoreType.DMA((bits,)),
            pltpu.SemaphoreType.DMA((bits,)),
            pltpu.SemaphoreType.DMA((CHUNKS,)),
            pltpu.SemaphoreType.DMA,
        ],
        compiler_params=pltpu.CompilerParams(
            collective_id=0, has_side_effects=True, vmem_limit_bytes=56 * 2**20
        ),
    )(slab, sketch)
    return pl.pallas_call(
        hand_over,
        out_shape=(
            jax.ShapeDtypeStruct((height, rank), F32),
            jax.ShapeDtypeStruct((rank, width), F32),
        ),
        in_specs=[anywhere] * 2,
        out_specs=(anywhere,) * 2,
        scratch_shapes=[
            pltpu.VMEM((height, rank), F32),
            pltpu.VMEM((rank // TILE, TILE, width), F32),
            pltpu.SemaphoreType.DMA((rank // TILE + 1,)),
            pltpu.SemaphoreType.DMA((rank // TILE + 1,)),
        ],
        compiler_params=pltpu.CompilerParams(vmem_limit_bytes=56 * 2**20),
    )(basis, projection)


def solution(mesh):
    rows, cols = mesh.shape["row"], mesh.shape["col"]
    placed = (P(("row", "col"), None), P())
    return jax.shard_map(
        functools.partial(per_device, rows, cols),
        mesh=mesh,
        in_specs=placed,
        out_specs=placed,
        check_vma=False,
    )
```

```python
import functools
import math

import jax
import jax.numpy as jnp
from jax import lax
from jax.experimental import pallas as pl
from jax.experimental.pallas import tpu as pltpu
from jax.sharding import PartitionSpec as P

MESH = pl.DeviceIdType.MESH
BF16 = jnp.bfloat16
F32 = jnp.float32
LANES = 128
TILE = 8
LOAD = 1024
CHUNKS = 8
STRIP = 512
SPACING = 2
GRAM_HOP = 2
PANEL = 32
CHOL = 8


def split(value):
    high = value.astype(BF16)
    return high, (value - high.astype(F32)).astype(BF16)


def bit_of(axis, bit):
    index = lax.axis_index(axis)
    value = (index // 2**bit) % 2
    return {axis: 2**bit * (1 - 2 * value)}, value


def orders(rows, cols):
    row_bits = [("row", b) for b in range(1, rows.bit_length() - 1)]
    col_bits = [("col", b) for b in range(cols.bit_length() - 1)]
    inner = 1 if len(col_bits) == 3 else len(col_bits) // 2
    near, far = col_bits[:inner], col_bits[inner:]
    core = [("row", 0)]
    even, odd = core + near + far[:1] + row_bits, core + row_bits + far[:1] + near
    return list(zip(even, odd)), [(b, b) for b in far[1:]]


def pick(even, odd):
    core = lax.axis_index("row") % 2
    device = {"row": lax.axis_index("row"), "col": lax.axis_index("col")}
    bit = 0
    for (axis, place), weight in ((even, 1 - core), (odd, core)):
        step, value = bit_of(axis, place)
        device[axis] = device[axis] + weight * step[axis]
        bit = bit + weight * value
    return (device["row"], device["col"]), bit


def sum_kernel(
    rows, cols, slab, sketch, basis_out, projection_out,
    staged, sk, high, low, part, landed, total, swap_in, swap_out, basis, left, grams, gram_in, work, panel, wide_acc,
    slab_sem, sk_sem, send_sem, recv_sem, gram_send, gram_recv, out_sem, basis_sem,
):
    height, width = slab.shape
    bits = (rows * cols).bit_length() - 1
    units = width // LANES * (LANES // TILE)
    chunks = CHUNKS
    chunk_units = units // chunks
    chunk_cols = width // chunks
    loads = width // LOAD

    sketch_copy = pltpu.make_async_copy(sketch, sk, sk_sem)
    sketch_copy.start()

    def load(i):
        return pltpu.make_async_copy(
            slab.at[:, pl.ds(pl.multiple_of(i * LOAD, LOAD), LOAD)], staged.at[i], slab_sem.at[i]
        )

    for i in range(loads):
        load(i).start()

    halving, swapping = orders(rows, cols)
    halves, swaps = len(halving), len(swapping)
    kept_units = chunk_units >> halves
    gram_order = [(even, even) for even, _ in halving + swapping]
    barrier = pltpu.get_barrier_semaphore()
    for place in gram_order:
        device, _ = pick(*place)
        pl.semaphore_signal(barrier, inc=1, device_id=device, device_id_type=MESH)

    wide_acc[...] = jnp.zeros_like(wide_acc)
    sketch_copy.wait()

    def sample(i, carry):
        load(i).wait()
        a_high, a_low = split(staged[i])
        columns = pl.ds(pl.multiple_of(i * LOAD, LOAD), LOAD)
        high[:, columns] = a_high
        low[:, columns] = a_low
        s_high, s_low = split(sk[columns, :])
        both = jnp.concatenate([s_high, s_low], axis=1)
        wide_acc[...] += jnp.dot(a_high, both, preferred_element_type=F32)
        wide_acc[:, :LANES] += jnp.dot(a_low, s_high, preferred_element_type=F32)
        return carry

    lax.fori_loop(0, loads, sample, 0)
    sampled = wide_acc[:, :LANES] + wide_acc[:, LANES:]
    basis[...] = sampled
    turned = sampled.T
    t_high, t_low = split(turned)
    left[:LANES, :] = t_high
    left[LANES:, :] = t_low
    grams[0] = jnp.dot(
        turned, sampled, precision=lax.Precision.HIGHEST, preferred_element_type=F32
    )
    pl.semaphore_wait(barrier, bits)

    per = LANES // TILE
    strips = chunk_cols // STRIP

    def product(k):
        for i in range(strips):
            columns = pl.ds(pl.multiple_of((k * strips + i) * STRIP, STRIP), STRIP)
            both = jnp.dot(left[...], high[:, columns], preferred_element_type=F32)
            more = jnp.dot(left[:LANES, :], low[:, columns], preferred_element_type=F32)
            value = both[:LANES] + both[LANES:] + more
            for j in range(STRIP // LANES):
                first = k * chunk_units + (i * (STRIP // LANES) + j) * per
                part[pl.ds(first, per)] = value[:, j * LANES : (j + 1) * LANES].reshape(
                    per, TILE, LANES
                )

    table, start = [], 0
    for s, places in enumerate(halving):
        device, bit = pick(*places)
        half = chunk_units >> (s + 1)
        table.append((device, start + bit * half, start + (1 - bit) * half))
        start = start + bit * half

    def place(k, s):
        device, keep, give = table[s]
        half = chunk_units >> (s + 1)
        base = k * chunk_units
        return device, base + keep, base + give, half, base + chunk_units - 2 * half

    def swap(k, s):
        if s == 0:
            source = part.at[pl.ds(place(k, halves - 1)[1], kept_units)]
        else:
            source = swap_out.at[k, s - 1]
        return pltpu.make_async_remote_copy(
            src_ref=source,
            dst_ref=swap_in.at[k, s],
            send_sem=send_sem.at[k, halves + s],
            recv_sem=recv_sem.at[k, halves + s],
            device_id=pick(*swapping[s])[0],
            device_id_type=MESH,
        )

    def scatter(k, s):
        device, _, give, half, slot = place(k, s)
        return pltpu.make_async_remote_copy(
            src_ref=part.at[pl.ds(give, half)],
            dst_ref=landed.at[pl.ds(slot, half)],
            send_sem=send_sem.at[k, s],
            recv_sem=recv_sem.at[k, s],
            device_id=device,
            device_id_type=MESH,
        )

    def gather(k, s):
        device, keep, _, half, _ = place(k, s)
        return pltpu.make_async_remote_copy(
            src_ref=total.at[pl.ds(keep, half)],
            dst_ref=total.at[pl.ds(keep, half)],
            send_sem=send_sem.at[k, 2 * halves + swaps - 1 - s],
            recv_sem=recv_sem.at[k, 2 * halves + swaps - 1 - s],
            device_id=device,
            device_id_type=MESH,
        )

    def exchange_gram(s):
        device, _ = pick(*gram_order[s])
        return pltpu.make_async_remote_copy(
            src_ref=grams.at[s],
            dst_ref=gram_in.at[s],
            send_sem=gram_send.at[s],
            recv_sem=gram_recv.at[s],
            device_id=device,
            device_id_type=MESH,
        )

    def deliver(k):
        return pltpu.make_async_copy(
            staged.at[k, pl.ds(0, LANES)],
            projection_out.at[:, pl.ds(pl.multiple_of(k * chunk_cols, chunk_cols), chunk_cols)],
            out_sem.at[k],
        )

    def apply(k):
        inverse = work[:, LANES:]
        i_high, i_low = split(inverse)
        doubled = jnp.concatenate([i_high, i_high], axis=1)
        for i in range(strips):
            first = k * chunk_units + i * (STRIP // LANES) * per
            value = jnp.concatenate(
                [
                    total[pl.ds(first + j * per, per)].reshape(LANES, LANES)
                    for j in range(STRIP // LANES)
                ],
                axis=1,
            )
            v_high, v_low = split(value)
            staged[k, :LANES, i * STRIP : (i + 1) * STRIP] = jnp.dot(
                doubled, jnp.concatenate([v_high, v_low], axis=0), preferred_element_type=F32
            ) + jnp.dot(i_low, v_high, preferred_element_type=F32)
        deliver(k).start()

    last = 2 * halves + swaps

    def chunk_step(k, s):
        if s == 0:
            product(k)
            scatter(k, 0).start()
        elif s <= halves:
            scatter(k, s - 1).wait_recv()
            _, keep, _, half, slot = place(k, s - 1)
            part[pl.ds(keep, half)] = part[pl.ds(keep, half)] + landed[pl.ds(slot, half)]
            if s < halves:
                scatter(k, s).start()
            else:
                swap(k, 0).start()
        elif s <= halves + swaps:
            i = s - halves - 1
            swap(k, i).wait_recv()
            keep = place(k, halves - 1)[1]
            mine = part[pl.ds(keep, kept_units)] if i == 0 else swap_out[k, i - 1]
            value = mine + swap_in[k, i]
            if i + 1 < swaps:
                swap_out[k, i] = value
                swap(k, i + 1).start()
            else:
                total[pl.ds(keep, kept_units)] = value
                gather(k, halves - 1).start()
        else:
            gather(k, last - s).wait_recv()
            if s < last:
                gather(k, last - s - 1).start()

    square_rows = lax.broadcasted_iota(jnp.int32, (LANES, LANES), 0)
    square_lanes = lax.broadcasted_iota(jnp.int32, (LANES, LANES), 1)
    panel_rows = lax.broadcasted_iota(jnp.int32, (PANEL, LANES), 0)
    panel_lanes = lax.broadcasted_iota(jnp.int32, (PANEL, LANES), 1)
    highest = lax.Precision.HIGHEST
    basis_copy = pltpu.make_async_copy(basis, basis_out, basis_sem)

    def gram_step(step):
        if step >= 1:
            exchange_gram(step - 1).wait_recv()
            grams[step] = grams[step - 1] + gram_in[step - 1]
        if step < bits:
            exchange_gram(step).start()
        else:
            work[:, :LANES] = grams[bits]
            work[:, LANES:] = (square_rows == square_lanes).astype(F32)

    def eliminate(base, piece):
        here = pl.ds(pl.multiple_of(base, PANEL), PANEL)
        if piece == 0:
            block = pltpu.roll(work[here, :LANES], (LANES - base) % LANES, 1)
            unit = (panel_rows + PANEL == panel_lanes).astype(F32)
            value = jnp.where(panel_lanes < PANEL, block, unit)
        else:
            value = panel[...]
        tiles = value.reshape(PANEL // TILE, TILE, LANES)
        tile_rows = panel_rows.reshape(PANEL // TILE, TILE, LANES)
        for j in range(piece * CHOL, (piece + 1) * CHOL):
            column = jnp.broadcast_to(tiles[:, :, j : j + 1], tiles.shape)
            here_j = (j // TILE, slice(j % TILE, j % TILE + 1))
            pivot = jnp.broadcast_to(column[here_j], (TILE, LANES))
            row = jnp.broadcast_to(tiles[here_j], (TILE, LANES))
            below = jnp.where(tile_rows > j, column, 0.0)
            tiles = tiles - below * (row * (1.0 / pivot))[None]
        value = tiles.reshape(PANEL, LANES)
        panel[...] = value
        if (piece + 1) * CHOL < PANEL:
            return
        diagonal = jnp.sum(
            jnp.where(panel_rows == panel_lanes, value, 0.0), axis=1, keepdims=True
        )
        value = pltpu.roll(value / jnp.sqrt(diagonal), (base + LANES - PANEL) % LANES, 1)
        inside = jnp.logical_and(panel_lanes >= base, panel_lanes < base + PANEL)
        value = jnp.where(inside, value, 0.0)
        done = jnp.dot(value, work[...], precision=highest, preferred_element_type=F32)
        work[here, :] = done
        change = jnp.dot(done[:, :LANES].T, done, precision=highest, preferred_element_type=F32)
        rest = lax.broadcasted_iota(jnp.int32, (LANES, 2 * LANES), 0) >= base + PANEL
        work[...] = jnp.where(rest, work[...] - change, work[...])

    def make_basis():
        product_turned = lax.dot_general(
            basis[...], work[:, LANES:], (((1,), (1,)), ((), ())),
            precision=highest, preferred_element_type=F32,
        )
        basis[...] = product_turned * math.sqrt(height * rows * cols)
        basis_copy.start()

    first_elimination = GRAM_HOP * bits + 1
    eliminations = LANES // CHOL
    hops = [2 if s == 0 or s > 2 else 3 for s in range(halves)]
    due_at = [0]
    for hop in hops + [3] * swaps + hops[::-1]:
        due_at.append(due_at[-1] + hop)
    apply_at = [
        max(due_at[-1] + SPACING * k, first_elimination + eliminations + 1 + k)
        for k in range(chunks)
    ]
    pieces = PANEL // CHOL

    def tick(t, carry):
        for step in range(bits + 1):
            pl.when(t == GRAM_HOP * step)(functools.partial(gram_step, step))
        for s in reversed(range(last + 1)):
            since = t - due_at[s]
            due = jnp.logical_and(since >= 0, since < SPACING * chunks)
            due = jnp.logical_and(due, since % SPACING == 0)
            pl.when(due)(functools.partial(chunk_step, since // SPACING, s))
        done = t - first_elimination
        for piece in range(pieces):
            due = jnp.logical_and(done >= 0, done < eliminations)
            base = done // pieces * PANEL
            pl.when(jnp.logical_and(due, done % pieces == piece))(
                functools.partial(eliminate, base, piece)
            )
        pl.when(done == eliminations)(make_basis)
        ready, finished = 0, 0
        for k, time in enumerate(apply_at):
            now = jnp.where(t == time, 1, 0)
            ready, finished = ready + now, finished + now * k
        pl.when(ready > 0)(functools.partial(apply, finished))
        return carry

    lax.fori_loop(0, apply_at[-1] + 1, tick, 0)

    def drain(k, carry):
        for s in range(halves):
            scatter(k, s).wait_send()
            gather(k, s).wait_send()
        for s in range(swaps):
            swap(k, s).wait_send()
        deliver(k).wait()
        return carry

    lax.fori_loop(0, chunks, drain, 0)
    basis_copy.wait()
    for s in range(bits):
        exchange_gram(s).wait_send()


def hand_over(basis, projection, basis_out, projection_out, basis_held, held, reads, writes):
    pieces, height, _ = held.shape
    moves = [(basis, basis_held, basis_out)]
    for i in range(pieces):
        band = pl.ds(i * height, height)
        moves.append((projection.at[band], held.at[i], projection_out.at[band]))
    for i, (source, middle, _) in enumerate(moves):
        pltpu.make_async_copy(source, middle, reads.at[i]).start()
    for i, (source, middle, target) in enumerate(moves):
        pltpu.make_async_copy(source, middle, reads.at[i]).wait()
        pltpu.make_async_copy(middle, target, writes.at[i]).start()
    for i, (_, middle, target) in enumerate(moves):
        pltpu.make_async_copy(middle, target, writes.at[i]).wait()


def per_device(rows, cols, slab, sketch):
    height, width = slab.shape
    rank = sketch.shape[1]
    bits = (rows * cols).bit_length() - 1
    units = width // LANES * (rank // TILE)
    halves, swaps = (len(part) for part in orders(rows, cols))
    kept = (units // CHUNKS) >> halves
    anywhere = pl.BlockSpec(memory_space=pl.ANY)
    basis, projection = pl.pallas_call(
        functools.partial(sum_kernel, rows, cols),
        out_shape=(
            jax.ShapeDtypeStruct((height, rank), F32),
            jax.ShapeDtypeStruct((rank, width), F32),
        ),
        in_specs=[anywhere] * 2,
        out_specs=(anywhere,) * 2,
        scratch_shapes=[
            pltpu.VMEM((width // LOAD, height, LOAD), F32),
            pltpu.VMEM((width, rank), F32),
            pltpu.VMEM((height, width), BF16),
            pltpu.VMEM((height, width), BF16),
            pltpu.VMEM((units, TILE, LANES), F32),
            pltpu.VMEM((units, TILE, LANES), F32),
            pltpu.VMEM((units, TILE, LANES), F32),
            pltpu.VMEM((CHUNKS, swaps, kept, TILE, LANES), F32),
            pltpu.VMEM((CHUNKS, swaps, kept, TILE, LANES), F32),
            pltpu.VMEM((height, rank), F32),
            pltpu.VMEM((2 * rank, height), BF16),
            pltpu.VMEM((bits + 1, rank, rank), F32),
            pltpu.VMEM((bits, rank, rank), F32),
            pltpu.VMEM((rank, 2 * rank), F32),
            pltpu.VMEM((PANEL, rank), F32),
            pltpu.VMEM((height, 2 * rank), F32),
            pltpu.SemaphoreType.DMA((width // LOAD,)),
            pltpu.SemaphoreType.DMA,
            pltpu.SemaphoreType.DMA((CHUNKS, 2 * halves + swaps)),
            pltpu.SemaphoreType.DMA((CHUNKS, 2 * halves + swaps)),
            pltpu.SemaphoreType.DMA((bits,)),
            pltpu.SemaphoreType.DMA((bits,)),
            pltpu.SemaphoreType.DMA((CHUNKS,)),
            pltpu.SemaphoreType.DMA,
        ],
        compiler_params=pltpu.CompilerParams(
            collective_id=0, has_side_effects=True, vmem_limit_bytes=56 * 2**20
        ),
    )(slab, sketch)
    return pl.pallas_call(
        hand_over,
        out_shape=(
            jax.ShapeDtypeStruct((height, rank), F32),
            jax.ShapeDtypeStruct((rank, width), F32),
        ),
        in_specs=[anywhere] * 2,
        out_specs=(anywhere,) * 2,
        scratch_shapes=[
            pltpu.VMEM((height, rank), F32),
            pltpu.VMEM((rank // TILE, TILE, width), F32),
            pltpu.SemaphoreType.DMA((rank // TILE + 1,)),
            pltpu.SemaphoreType.DMA((rank // TILE + 1,)),
        ],
        compiler_params=pltpu.CompilerParams(vmem_limit_bytes=56 * 2**20),
    )(basis, projection)


def solution(mesh):
    rows, cols = mesh.shape["row"], mesh.shape["col"]
    placed = (P(("row", "col"), None), P())
    return jax.shard_map(
        functools.partial(per_device, rows, cols),
        mesh=mesh,
        in_specs=placed,
        out_specs=placed,
        check_vma=False,
    )
```

```python
import functools
import math

import jax
import jax.numpy as jnp
from jax import lax
from jax.experimental import pallas as pl
from jax.experimental.pallas import tpu as pltpu
from jax.sharding import PartitionSpec as P

MESH = pl.DeviceIdType.MESH
BF16 = jnp.bfloat16
F32 = jnp.float32
LANES = 128
TILE = 8
LOAD = 1024
CHUNKS = 8
STRIP = 512
PIECE = 16
MOST_PIECES = 4
SPACING = 2
GRAM_HOP = 2
PANEL = 32
CHOL = 8


def split(value):
    high = value.astype(BF16)
    return high, (value - high.astype(F32)).astype(BF16)


def bit_of(axis, bit):
    index = lax.axis_index(axis)
    value = (index // 2**bit) % 2
    return {axis: 2**bit * (1 - 2 * value)}, value


def orders(rows, cols):
    row_bits = [("row", b) for b in range(1, rows.bit_length() - 1)]
    col_bits = [("col", b) for b in range(cols.bit_length() - 1)]
    inner = 1 if len(col_bits) == 3 else len(col_bits) // 2
    near, far = col_bits[:inner], col_bits[inner:]
    core = [("row", 0)]
    even, odd = core + near + far[:1] + row_bits, core + row_bits + far[:1] + near
    return list(zip(even, odd)), [(b, b) for b in far[1:]]


def pick(even, odd):
    core = lax.axis_index("row") % 2
    device = {"row": lax.axis_index("row"), "col": lax.axis_index("col")}
    bit = 0
    for (axis, place), weight in ((even, 1 - core), (odd, core)):
        step, value = bit_of(axis, place)
        device[axis] = device[axis] + weight * step[axis]
        bit = bit + weight * value
    return (device["row"], device["col"]), bit


def sum_kernel(
    rows, cols, slab, sketch, basis_out, projection_out,
    staged, sk, high, low, part, landed, total, swap_in, swap_out, basis, left, grams, gram_in, work, panel, wide_acc,
    slab_sem, sk_sem, send_sem, recv_sem, gram_send, gram_recv, out_sem, basis_sem,
):
    height, width = slab.shape
    bits = (rows * cols).bit_length() - 1
    units = width // LANES * (LANES // TILE)
    chunks = CHUNKS
    chunk_units = units // chunks
    chunk_cols = width // chunks
    loads = width // LOAD

    def load_sketch(i):
        band = pl.ds(i * LOAD, LOAD)
        return pltpu.make_async_copy(sketch.at[band], sk.at[band], sk_sem.at[i])

    def load(i):
        return pltpu.make_async_copy(
            slab.at[:, pl.ds(pl.multiple_of(i * LOAD, LOAD), LOAD)], staged.at[i], slab_sem.at[i]
        )

    for i in range(loads):
        load_sketch(i).start()
        load(i).start()

    halving, swapping = orders(rows, cols)
    halves, swaps = len(halving), len(swapping)
    kept_units = chunk_units >> halves
    gram_order = [(even, even) for even, _ in halving + swapping]
    barrier = pltpu.get_barrier_semaphore()
    for place in gram_order:
        device, _ = pick(*place)
        pl.semaphore_signal(barrier, inc=1, device_id=device, device_id_type=MESH)

    wide_acc[...] = jnp.zeros_like(wide_acc)

    def multiply(i):
        columns = slice(i * LOAD, (i + 1) * LOAD)
        s_high, s_low = split(sk[columns, :])
        both = jnp.concatenate([s_high, s_low], axis=1)
        wide_acc[...] += jnp.dot(high[:, columns], both, preferred_element_type=F32)
        wide_acc[:, :LANES] += jnp.dot(low[:, columns], s_high, preferred_element_type=F32)

    for i in range(loads + 1):
        if i < loads:
            load_sketch(i).wait()
            load(i).wait()
            columns = slice(i * LOAD, (i + 1) * LOAD)
            high[:, columns], low[:, columns] = split(staged[i])
        if i:
            multiply(i - 1)

    sampled = wide_acc[:, :LANES] + wide_acc[:, LANES:]
    basis[...] = sampled
    turned = sampled.T
    t_high, t_low = split(turned)
    left[:LANES, :] = t_high
    left[LANES:, :] = t_low
    grams[0] = jnp.dot(
        turned, sampled, precision=lax.Precision.HIGHEST, preferred_element_type=F32
    )
    pl.semaphore_wait(barrier, bits)

    per = LANES // TILE
    strips = chunk_cols // STRIP

    def product(k):
        for i in range(strips):
            columns = pl.ds(pl.multiple_of((k * strips + i) * STRIP, STRIP), STRIP)
            both = jnp.dot(left[...], high[:, columns], preferred_element_type=F32)
            more = jnp.dot(left[:LANES, :], low[:, columns], preferred_element_type=F32)
            value = both[:LANES] + both[LANES:] + more
            for j in range(STRIP // LANES):
                first = k * chunk_units + (i * (STRIP // LANES) + j) * per
                part[pl.ds(first, per)] = value[:, j * LANES : (j + 1) * LANES].reshape(
                    per, TILE, LANES
                )

    table, start = [], 0
    for s, places in enumerate(halving):
        device, bit = pick(*places)
        half = chunk_units >> (s + 1)
        table.append((device, start + bit * half, start + (1 - bit) * half))
        start = start + bit * half

    def place(k, s):
        device, keep, give = table[s]
        half = chunk_units >> (s + 1)
        base = k * chunk_units
        return device, base + keep, base + give, half, base + chunk_units - 2 * half

    def swap(k, s):
        if s == 0:
            source = part.at[pl.ds(place(k, halves - 1)[1], kept_units)]
        else:
            source = swap_out.at[k, s - 1]
        return pltpu.make_async_remote_copy(
            src_ref=source,
            dst_ref=swap_in.at[k, s],
            send_sem=send_sem.at[k, halves + s, 0],
            recv_sem=recv_sem.at[k, halves + s, 0],
            device_id=pick(*swapping[s])[0],
            device_id_type=MESH,
        )

    class Pieces:
        def __init__(self, copies):
            self.copies = copies

        def start(self):
            for copy in self.copies:
                copy.start()

        def wait_recv(self):
            for copy in self.copies:
                copy.wait_recv()

        def wait_send(self):
            for copy in self.copies:
                copy.wait_send()

    def cut(device, source, source_at, target, target_at, size, k, index):
        pieces = min(MOST_PIECES, max(1, size // PIECE))
        each = size // pieces
        return Pieces(
            [
                pltpu.make_async_remote_copy(
                    src_ref=source.at[pl.ds(source_at + p * each, each)],
                    dst_ref=target.at[pl.ds(target_at + p * each, each)],
                    send_sem=send_sem.at[k, index, p],
                    recv_sem=recv_sem.at[k, index, p],
                    device_id=device,
                    device_id_type=MESH,
                )
                for p in range(pieces)
            ]
        )

    def scatter(k, s):
        device, _, give, half, slot = place(k, s)
        return cut(device, part, give, landed, slot, half, k, s)

    def gather(k, s):
        device, keep, _, half, _ = place(k, s)
        return cut(device, total, keep, total, keep, half, k, 2 * halves + swaps - 1 - s)

    def exchange_gram(s):
        device, _ = pick(*gram_order[s])
        return pltpu.make_async_remote_copy(
            src_ref=grams.at[s],
            dst_ref=gram_in.at[s],
            send_sem=gram_send.at[s],
            recv_sem=gram_recv.at[s],
            device_id=device,
            device_id_type=MESH,
        )

    def deliver(k):
        return pltpu.make_async_copy(
            staged.at[k, pl.ds(0, LANES)],
            projection_out.at[:, pl.ds(pl.multiple_of(k * chunk_cols, chunk_cols), chunk_cols)],
            out_sem.at[k],
        )

    def apply(k):
        inverse = work[:, LANES:]
        i_high, i_low = split(inverse)
        doubled = jnp.concatenate([i_high, i_high], axis=1)
        for i in range(strips):
            first = k * chunk_units + i * (STRIP // LANES) * per
            value = jnp.concatenate(
                [
                    total[pl.ds(first + j * per, per)].reshape(LANES, LANES)
                    for j in range(STRIP // LANES)
                ],
                axis=1,
            )
            v_high, v_low = split(value)
            staged[k, :LANES, i * STRIP : (i + 1) * STRIP] = jnp.dot(
                doubled, jnp.concatenate([v_high, v_low], axis=0), preferred_element_type=F32
            ) + jnp.dot(i_low, v_high, preferred_element_type=F32)
        deliver(k).start()

    last = 2 * halves + swaps

    def chunk_step(k, s):
        if s == 0:
            product(k)
            scatter(k, 0).start()
        elif s <= halves:
            scatter(k, s - 1).wait_recv()
            _, keep, _, half, slot = place(k, s - 1)
            part[pl.ds(keep, half)] = part[pl.ds(keep, half)] + landed[pl.ds(slot, half)]
            if s < halves:
                scatter(k, s).start()
            else:
                swap(k, 0).start()
        elif s <= halves + swaps:
            i = s - halves - 1
            swap(k, i).wait_recv()
            keep = place(k, halves - 1)[1]
            mine = part[pl.ds(keep, kept_units)] if i == 0 else swap_out[k, i - 1]
            value = mine + swap_in[k, i]
            if i + 1 < swaps:
                swap_out[k, i] = value
                swap(k, i + 1).start()
            else:
                total[pl.ds(keep, kept_units)] = value
                gather(k, halves - 1).start()
        else:
            gather(k, last - s).wait_recv()
            if s < last:
                gather(k, last - s - 1).start()

    square_rows = lax.broadcasted_iota(jnp.int32, (LANES, LANES), 0)
    square_lanes = lax.broadcasted_iota(jnp.int32, (LANES, LANES), 1)
    panel_rows = lax.broadcasted_iota(jnp.int32, (PANEL, LANES), 0)
    panel_lanes = lax.broadcasted_iota(jnp.int32, (PANEL, LANES), 1)
    highest = lax.Precision.HIGHEST
    basis_copy = pltpu.make_async_copy(basis, basis_out, basis_sem)

    def gram_step(step):
        if step >= 1:
            exchange_gram(step - 1).wait_recv()
            grams[step] = grams[step - 1] + gram_in[step - 1]
        if step < bits:
            exchange_gram(step).start()
        else:
            work[:, :LANES] = grams[bits]
            work[:, LANES:] = (square_rows == square_lanes).astype(F32)

    def eliminate(base, piece):
        here = pl.ds(pl.multiple_of(base, PANEL), PANEL)
        if piece == 0:
            block = pltpu.roll(work[here, :LANES], (LANES - base) % LANES, 1)
            unit = (panel_rows + PANEL == panel_lanes).astype(F32)
            value = jnp.where(panel_lanes < PANEL, block, unit)
        else:
            value = panel[...]
        for j in range(piece * CHOL, (piece + 1) * CHOL, 2):
            first = jnp.broadcast_to(value[:, j : j + 1], (PANEL, LANES))
            second = jnp.broadcast_to(value[:, j + 1 : j + 2], (PANEL, LANES))
            ratio = first[j + 1 : j + 2, :] / first[j : j + 1, :]
            top = value[j : j + 1, :]
            next_row = value[j + 1 : j + 2, :] - ratio * top
            pivot = second[j + 1 : j + 2, :] - ratio * first[j + 1 : j + 2, :]
            change = first * (top / first[j : j + 1, :]) + (second - first * ratio) * (
                next_row / pivot
            )
            value = jnp.where(panel_rows > j + 1, value - change, value)
            value = jnp.where(panel_rows == j + 1, next_row, value)
        panel[...] = value
        if (piece + 1) * CHOL < PANEL:
            return
        diagonal = jnp.sum(
            jnp.where(panel_rows == panel_lanes, value, 0.0), axis=1, keepdims=True
        )
        value = pltpu.roll(value / jnp.sqrt(diagonal), (base + LANES - PANEL) % LANES, 1)
        inside = jnp.logical_and(panel_lanes >= base, panel_lanes < base + PANEL)
        value = jnp.where(inside, value, 0.0)
        done = jnp.dot(value, work[...], precision=highest, preferred_element_type=F32)
        work[here, :] = done
        change = jnp.dot(done[:, :LANES].T, done, precision=highest, preferred_element_type=F32)
        rest = lax.broadcasted_iota(jnp.int32, (LANES, 2 * LANES), 0) >= base + PANEL
        work[...] = jnp.where(rest, work[...] - change, work[...])

    def make_basis():
        product_turned = lax.dot_general(
            basis[...], work[:, LANES:], (((1,), (1,)), ((), ())),
            precision=highest, preferred_element_type=F32,
        )
        basis[...] = product_turned * math.sqrt(height * rows * cols)
        basis_copy.start()

    first_elimination = GRAM_HOP * bits + 1
    eliminations = LANES // CHOL
    hops = [2 if s == 0 or s > 2 else 3 for s in range(halves)]
    due_at = [0]
    for hop in hops + [3] * swaps + hops[::-1]:
        due_at.append(due_at[-1] + hop)
    apply_at = [
        max(due_at[-1] + SPACING * k, first_elimination + eliminations + 1 + k)
        for k in range(chunks)
    ]
    pieces = PANEL // CHOL

    def tick(t, carry):
        for step in range(bits + 1):
            pl.when(t == GRAM_HOP * step)(functools.partial(gram_step, step))
        for s in reversed(range(last + 1)):
            since = t - due_at[s]
            due = jnp.logical_and(since >= 0, since < SPACING * chunks)
            due = jnp.logical_and(due, since % SPACING == 0)
            pl.when(due)(functools.partial(chunk_step, since // SPACING, s))
        done = t - first_elimination
        for piece in range(pieces):
            due = jnp.logical_and(done >= 0, done < eliminations)
            base = done // pieces * PANEL
            pl.when(jnp.logical_and(due, done % pieces == piece))(
                functools.partial(eliminate, base, piece)
            )
        pl.when(done == eliminations)(make_basis)
        ready, finished = 0, 0
        for k, time in enumerate(apply_at):
            now = jnp.where(t == time, 1, 0)
            ready, finished = ready + now, finished + now * k
        pl.when(ready > 0)(functools.partial(apply, finished))
        return carry

    lax.fori_loop(0, apply_at[-1] + 1, tick, 0)

    def drain(k, carry):
        for s in range(halves):
            scatter(k, s).wait_send()
            gather(k, s).wait_send()
        for s in range(swaps):
            swap(k, s).wait_send()
        deliver(k).wait()
        return carry

    lax.fori_loop(0, chunks, drain, 0)
    basis_copy.wait()
    for s in range(bits):
        exchange_gram(s).wait_send()


def hand_over(basis, projection, basis_out, projection_out, basis_held, held, reads, writes):
    pieces, height, _ = held.shape
    moves = [(basis, basis_held, basis_out)]
    for i in range(pieces):
        band = pl.ds(i * height, height)
        moves.append((projection.at[band], held.at[i], projection_out.at[band]))
    for i, (source, middle, _) in enumerate(moves):
        pltpu.make_async_copy(source, middle, reads.at[i]).start()
    for i, (source, middle, target) in enumerate(moves):
        pltpu.make_async_copy(source, middle, reads.at[i]).wait()
        pltpu.make_async_copy(middle, target, writes.at[i]).start()
    for i, (_, middle, target) in enumerate(moves):
        pltpu.make_async_copy(middle, target, writes.at[i]).wait()


def per_device(rows, cols, slab, sketch):
    height, width = slab.shape
    rank = sketch.shape[1]
    bits = (rows * cols).bit_length() - 1
    units = width // LANES * (rank // TILE)
    halves, swaps = (len(part) for part in orders(rows, cols))
    kept = (units // CHUNKS) >> halves
    anywhere = pl.BlockSpec(memory_space=pl.ANY)
    basis, projection = pl.pallas_call(
        functools.partial(sum_kernel, rows, cols),
        out_shape=(
            jax.ShapeDtypeStruct((height, rank), F32),
            jax.ShapeDtypeStruct((rank, width), F32),
        ),
        in_specs=[anywhere] * 2,
        out_specs=(anywhere,) * 2,
        scratch_shapes=[
            pltpu.VMEM((width // LOAD, height, LOAD), F32),
            pltpu.VMEM((width, rank), F32),
            pltpu.VMEM((height, width), BF16),
            pltpu.VMEM((height, width), BF16),
            pltpu.VMEM((units, TILE, LANES), F32),
            pltpu.VMEM((units, TILE, LANES), F32),
            pltpu.VMEM((units, TILE, LANES), F32),
            pltpu.VMEM((CHUNKS, swaps, kept, TILE, LANES), F32),
            pltpu.VMEM((CHUNKS, swaps, kept, TILE, LANES), F32),
            pltpu.VMEM((height, rank), F32),
            pltpu.VMEM((2 * rank, height), BF16),
            pltpu.VMEM((bits + 1, rank, rank), F32),
            pltpu.VMEM((bits, rank, rank), F32),
            pltpu.VMEM((rank, 2 * rank), F32),
            pltpu.VMEM((PANEL, rank), F32),
            pltpu.VMEM((height, 2 * rank), F32),
            pltpu.SemaphoreType.DMA((width // LOAD,)),
            pltpu.SemaphoreType.DMA((width // LOAD,)),
            pltpu.SemaphoreType.DMA((CHUNKS, 2 * halves + swaps, MOST_PIECES)),
            pltpu.SemaphoreType.DMA((CHUNKS, 2 * halves + swaps, MOST_PIECES)),
            pltpu.SemaphoreType.DMA((bits,)),
            pltpu.SemaphoreType.DMA((bits,)),
            pltpu.SemaphoreType.DMA((CHUNKS,)),
            pltpu.SemaphoreType.DMA,
        ],
        compiler_params=pltpu.CompilerParams(
            collective_id=0, has_side_effects=True, vmem_limit_bytes=56 * 2**20
        ),
    )(slab, sketch)
    return pl.pallas_call(
        hand_over,
        out_shape=(
            jax.ShapeDtypeStruct((height, rank), F32),
            jax.ShapeDtypeStruct((rank, width), F32),
        ),
        in_specs=[anywhere] * 2,
        out_specs=(anywhere,) * 2,
        scratch_shapes=[
            pltpu.VMEM((height, rank), F32),
            pltpu.VMEM((rank // TILE, TILE, width), F32),
            pltpu.SemaphoreType.DMA((rank // TILE + 1,)),
            pltpu.SemaphoreType.DMA((rank // TILE + 1,)),
        ],
        compiler_params=pltpu.CompilerParams(vmem_limit_bytes=56 * 2**20),
    )(basis, projection)


def solution(mesh):
    rows, cols = mesh.shape["row"], mesh.shape["col"]
    placed = (P(("row", "col"), None), P())
    return jax.shard_map(
        functools.partial(per_device, rows, cols),
        mesh=mesh,
        in_specs=placed,
        out_specs=placed,
        check_vma=False,
    )
```

```python
import functools
import math

import jax
import jax.numpy as jnp
from jax import lax
from jax.experimental import pallas as pl
from jax.experimental.pallas import tpu as pltpu
from jax.sharding import PartitionSpec as P

MESH = pl.DeviceIdType.MESH
BF16 = jnp.bfloat16
F32 = jnp.float32
LANES = 128
TILE = 8
LOAD = 2048
CHUNKS = 4
STRIP = 512
SPACING = 2
GRAM_HOP = 2
PANEL = 32
CHOL = 16


def split(value):
    high = value.astype(BF16)
    return high, (value - high.astype(F32)).astype(BF16)


def bit_of(axis, bit):
    index = lax.axis_index(axis)
    value = (index // 2**bit) % 2
    return {axis: 2**bit * (1 - 2 * value)}, value


def orders(rows, cols):
    row_bits = [("row", b) for b in range(1, rows.bit_length() - 1)]
    col_bits = [("col", b) for b in range(cols.bit_length() - 1)]
    inner = 1 if len(col_bits) == 3 else len(col_bits) // 2
    near, far = col_bits[:inner], col_bits[inner:]
    core = [("row", 0)]
    even, odd = core + near + far[:1] + row_bits, core + row_bits + far[:1] + near
    return list(zip(even, odd)), [(b, b) for b in far[1:]]


def pick(even, odd):
    core = lax.axis_index("row") % 2
    device = {"row": lax.axis_index("row"), "col": lax.axis_index("col")}
    bit = 0
    for (axis, place), weight in ((even, 1 - core), (odd, core)):
        step, value = bit_of(axis, place)
        device[axis] = device[axis] + weight * step[axis]
        bit = bit + weight * value
    return (device["row"], device["col"]), bit


def sum_kernel(
    rows, cols, slab, sketch, basis_out, projection_out,
    staged, sk, high, low, part, landed, total, swap_in, swap_out, basis, left, grams, gram_in, work, panel, wide_acc,
    slab_sem, sk_sem, send_sem, recv_sem, gram_send, gram_recv, out_sem, basis_sem,
):
    height, width = slab.shape
    bits = (rows * cols).bit_length() - 1
    units = width // LANES * (LANES // TILE)
    chunks = CHUNKS
    chunk_units = units // chunks
    chunk_cols = width // chunks
    loads = width // LOAD

    sketch_copy = pltpu.make_async_copy(sketch, sk, sk_sem)
    sketch_copy.start()

    def load(i):
        return pltpu.make_async_copy(
            slab.at[:, pl.ds(pl.multiple_of(i * LOAD, LOAD), LOAD)], staged.at[i], slab_sem.at[i]
        )

    for i in range(loads):
        load(i).start()

    halving, swapping = orders(rows, cols)
    halves, swaps = len(halving), len(swapping)
    kept_units = chunk_units >> halves
    gram_order = [(even, even) for even, _ in halving + swapping]
    barrier = pltpu.get_barrier_semaphore()
    for place in gram_order:
        device, _ = pick(*place)
        pl.semaphore_signal(barrier, inc=1, device_id=device, device_id_type=MESH)

    wide_acc[...] = jnp.zeros_like(wide_acc)
    sketch_copy.wait()

    def sample(i, carry):
        load(i).wait()
        a_high, a_low = split(staged[i])
        columns = pl.ds(pl.multiple_of(i * LOAD, LOAD), LOAD)
        high[:, columns] = a_high
        low[:, columns] = a_low
        s_high, s_low = split(sk[columns, :])
        both = jnp.concatenate([s_high, s_low], axis=1)
        wide_acc[...] += jnp.dot(a_high, both, preferred_element_type=F32)
        wide_acc[:, :LANES] += jnp.dot(a_low, s_high, preferred_element_type=F32)
        return carry

    lax.fori_loop(0, loads, sample, 0)
    sampled = wide_acc[:, :LANES] + wide_acc[:, LANES:]
    basis[...] = sampled
    turned = sampled.T
    t_high, t_low = split(turned)
    left[:LANES, :] = t_high
    left[LANES:, :] = t_low
    grams[0] = jnp.dot(
        turned, sampled, precision=lax.Precision.HIGHEST, preferred_element_type=F32
    )
    pl.semaphore_wait(barrier, bits)

    per = LANES // TILE
    strips = chunk_cols // STRIP

    def product(k):
        for i in range(strips):
            columns = pl.ds(pl.multiple_of((k * strips + i) * STRIP, STRIP), STRIP)
            both = jnp.dot(left[...], high[:, columns], preferred_element_type=F32)
            more = jnp.dot(left[:LANES, :], low[:, columns], preferred_element_type=F32)
            value = both[:LANES] + both[LANES:] + more
            for j in range(STRIP // LANES):
                first = k * chunk_units + (i * (STRIP // LANES) + j) * per
                part[pl.ds(first, per)] = value[:, j * LANES : (j + 1) * LANES].reshape(
                    per, TILE, LANES
                )

    table, start = [], 0
    for s, places in enumerate(halving):
        device, bit = pick(*places)
        half = chunk_units >> (s + 1)
        table.append((device, start + bit * half, start + (1 - bit) * half))
        start = start + bit * half

    def place(k, s):
        device, keep, give = table[s]
        half = chunk_units >> (s + 1)
        base = k * chunk_units
        return device, base + keep, base + give, half, base + chunk_units - 2 * half

    def swap(k, s):
        if s == 0:
            source = part.at[pl.ds(place(k, halves - 1)[1], kept_units)]
        else:
            source = swap_out.at[k, s - 1]
        return pltpu.make_async_remote_copy(
            src_ref=source,
            dst_ref=swap_in.at[k, s],
            send_sem=send_sem.at[k, halves + s],
            recv_sem=recv_sem.at[k, halves + s],
            device_id=pick(*swapping[s])[0],
            device_id_type=MESH,
        )

    def scatter(k, s):
        device, _, give, half, slot = place(k, s)
        return pltpu.make_async_remote_copy(
            src_ref=part.at[pl.ds(give, half)],
            dst_ref=landed.at[pl.ds(slot, half)],
            send_sem=send_sem.at[k, s],
            recv_sem=recv_sem.at[k, s],
            device_id=device,
            device_id_type=MESH,
        )

    def gather(k, s):
        device, keep, _, half, _ = place(k, s)
        return pltpu.make_async_remote_copy(
            src_ref=total.at[pl.ds(keep, half)],
            dst_ref=total.at[pl.ds(keep, half)],
            send_sem=send_sem.at[k, 2 * halves + swaps - 1 - s],
            recv_sem=recv_sem.at[k, 2 * halves + swaps - 1 - s],
            device_id=device,
            device_id_type=MESH,
        )

    def exchange_gram(s):
        device, _ = pick(*gram_order[s])
        return pltpu.make_async_remote_copy(
            src_ref=grams.at[s],
            dst_ref=gram_in.at[s],
            send_sem=gram_send.at[s],
            recv_sem=gram_recv.at[s],
            device_id=device,
            device_id_type=MESH,
        )

    def deliver(k):
        return pltpu.make_async_copy(
            staged.at[k, pl.ds(0, LANES)],
            projection_out.at[:, pl.ds(pl.multiple_of(k * chunk_cols, chunk_cols), chunk_cols)],
            out_sem.at[k],
        )

    def apply(k):
        inverse = work[:, LANES:]
        i_high, i_low = split(inverse)
        doubled = jnp.concatenate([i_high, i_high], axis=1)
        for i in range(strips):
            first = k * chunk_units + i * (STRIP // LANES) * per
            value = jnp.concatenate(
                [
                    total[pl.ds(first + j * per, per)].reshape(LANES, LANES)
                    for j in range(STRIP // LANES)
                ],
                axis=1,
            )
            v_high, v_low = split(value)
            staged[k, :LANES, i * STRIP : (i + 1) * STRIP] = jnp.dot(
                doubled, jnp.concatenate([v_high, v_low], axis=0), preferred_element_type=F32
            ) + jnp.dot(i_low, v_high, preferred_element_type=F32)
        deliver(k).start()

    last = 2 * halves + swaps

    def chunk_step(k, s):
        if s == 0:
            product(k)
            scatter(k, 0).start()
        elif s <= halves:
            scatter(k, s - 1).wait_recv()
            _, keep, _, half, slot = place(k, s - 1)
            part[pl.ds(keep, half)] = part[pl.ds(keep, half)] + landed[pl.ds(slot, half)]
            if s < halves:
                scatter(k, s).start()
            else:
                swap(k, 0).start()
        elif s <= halves + swaps:
            i = s - halves - 1
            swap(k, i).wait_recv()
            keep = place(k, halves - 1)[1]
            mine = part[pl.ds(keep, kept_units)] if i == 0 else swap_out[k, i - 1]
            value = mine + swap_in[k, i]
            if i + 1 < swaps:
                swap_out[k, i] = value
                swap(k, i + 1).start()
            else:
                total[pl.ds(keep, kept_units)] = value
                gather(k, halves - 1).start()
        else:
            gather(k, last - s).wait_recv()
            if s < last:
                gather(k, last - s - 1).start()

    square_rows = lax.broadcasted_iota(jnp.int32, (LANES, LANES), 0)
    square_lanes = lax.broadcasted_iota(jnp.int32, (LANES, LANES), 1)
    panel_rows = lax.broadcasted_iota(jnp.int32, (PANEL, LANES), 0)
    panel_lanes = lax.broadcasted_iota(jnp.int32, (PANEL, LANES), 1)
    highest = lax.Precision.HIGHEST
    basis_copy = pltpu.make_async_copy(basis, basis_out, basis_sem)

    def gram_step(step):
        if step >= 1:
            exchange_gram(step - 1).wait_recv()
            grams[step] = grams[step - 1] + gram_in[step - 1]
        if step < bits:
            exchange_gram(step).start()
        else:
            work[:, :LANES] = grams[bits]
            work[:, LANES:] = (square_rows == square_lanes).astype(F32)

    def eliminate(base, piece):
        here = pl.ds(pl.multiple_of(base, PANEL), PANEL)
        if piece == 0:
            block = pltpu.roll(work[here, :LANES], (LANES - base) % LANES, 1)
            unit = (panel_rows + PANEL == panel_lanes).astype(F32)
            value = jnp.where(panel_lanes < PANEL, block, unit)
        else:
            value = panel[...]
        for j in range(piece * CHOL, (piece + 1) * CHOL, 2):
            first = jnp.broadcast_to(value[:, j : j + 1], (PANEL, LANES))
            second = jnp.broadcast_to(value[:, j + 1 : j + 2], (PANEL, LANES))
            ratio = first[j + 1 : j + 2, :] / first[j : j + 1, :]
            top = value[j : j + 1, :]
            next_row = value[j + 1 : j + 2, :] - ratio * top
            pivot = second[j + 1 : j + 2, :] - ratio * first[j + 1 : j + 2, :]
            change = first * (top / first[j : j + 1, :]) + (second - first * ratio) * (
                next_row / pivot
            )
            value = jnp.where(panel_rows > j + 1, value - change, value)
            value = jnp.where(panel_rows == j + 1, next_row, value)
        panel[...] = value
        if (piece + 1) * CHOL < PANEL:
            return
        diagonal = jnp.sum(
            jnp.where(panel_rows == panel_lanes, value, 0.0), axis=1, keepdims=True
        )
        value = pltpu.roll(value / jnp.sqrt(diagonal), (base + LANES - PANEL) % LANES, 1)
        inside = jnp.logical_and(panel_lanes >= base, panel_lanes < base + PANEL)
        value = jnp.where(inside, value, 0.0)
        done = jnp.dot(value, work[...], precision=highest, preferred_element_type=F32)
        work[here, :] = done
        change = jnp.dot(done[:, :LANES].T, done, precision=highest, preferred_element_type=F32)
        rest = lax.broadcasted_iota(jnp.int32, (LANES, 2 * LANES), 0) >= base + PANEL
        work[...] = jnp.where(rest, work[...] - change, work[...])

    def make_basis():
        product_turned = lax.dot_general(
            basis[...], work[:, LANES:], (((1,), (1,)), ((), ())),
            precision=highest, preferred_element_type=F32,
        )
        basis[...] = product_turned * math.sqrt(height * rows * cols)
        basis_copy.start()

    first_elimination = GRAM_HOP * bits + 1
    eliminations = LANES // CHOL
    hops = [2 if s == 0 or s > 2 else 3 for s in range(halves)]
    due_at = [0]
    for hop in hops + [3] * swaps + hops[::-1]:
        due_at.append(due_at[-1] + hop)
    apply_at = [
        max(due_at[-1] + SPACING * k, first_elimination + eliminations + 1 + k)
        for k in range(chunks)
    ]
    pieces = PANEL // CHOL

    def tick(t, carry):
        for step in range(bits + 1):
            pl.when(t == GRAM_HOP * step)(functools.partial(gram_step, step))
        for s in reversed(range(last + 1)):
            since = t - due_at[s]
            due = jnp.logical_and(since >= 0, since < SPACING * chunks)
            due = jnp.logical_and(due, since % SPACING == 0)
            pl.when(due)(functools.partial(chunk_step, since // SPACING, s))
        done = t - first_elimination
        for piece in range(pieces):
            due = jnp.logical_and(done >= 0, done < eliminations)
            base = done // pieces * PANEL
            pl.when(jnp.logical_and(due, done % pieces == piece))(
                functools.partial(eliminate, base, piece)
            )
        pl.when(done == eliminations)(make_basis)
        ready, finished = 0, 0
        for k, time in enumerate(apply_at):
            now = jnp.where(t == time, 1, 0)
            ready, finished = ready + now, finished + now * k
        pl.when(ready > 0)(functools.partial(apply, finished))
        return carry

    lax.fori_loop(0, apply_at[-1] + 1, tick, 0)

    def drain(k, carry):
        for s in range(halves):
            scatter(k, s).wait_send()
            gather(k, s).wait_send()
        for s in range(swaps):
            swap(k, s).wait_send()
        deliver(k).wait()
        return carry

    lax.fori_loop(0, chunks, drain, 0)
    basis_copy.wait()
    for s in range(bits):
        exchange_gram(s).wait_send()


def hand_over(basis, projection, basis_out, projection_out, basis_held, held, reads, writes):
    pieces, height, _ = held.shape
    moves = [(basis, basis_held, basis_out)]
    for i in range(pieces):
        band = pl.ds(i * height, height)
        moves.append((projection.at[band], held.at[i], projection_out.at[band]))
    for i, (source, middle, _) in enumerate(moves):
        pltpu.make_async_copy(source, middle, reads.at[i]).start()
    for i, (source, middle, target) in enumerate(moves):
        pltpu.make_async_copy(source, middle, reads.at[i]).wait()
        pltpu.make_async_copy(middle, target, writes.at[i]).start()
    for i, (_, middle, target) in enumerate(moves):
        pltpu.make_async_copy(middle, target, writes.at[i]).wait()


def per_device(rows, cols, slab, sketch):
    height, width = slab.shape
    rank = sketch.shape[1]
    bits = (rows * cols).bit_length() - 1
    units = width // LANES * (rank // TILE)
    halves, swaps = (len(part) for part in orders(rows, cols))
    kept = (units // CHUNKS) >> halves
    anywhere = pl.BlockSpec(memory_space=pl.ANY)
    basis, projection = pl.pallas_call(
        functools.partial(sum_kernel, rows, cols),
        out_shape=(
            jax.ShapeDtypeStruct((height, rank), F32),
            jax.ShapeDtypeStruct((rank, width), F32),
        ),
        in_specs=[anywhere] * 2,
        out_specs=(anywhere,) * 2,
        scratch_shapes=[
            pltpu.VMEM((width // LOAD, height, LOAD), F32),
            pltpu.VMEM((width, rank), F32),
            pltpu.VMEM((height, width), BF16),
            pltpu.VMEM((height, width), BF16),
            pltpu.VMEM((units, TILE, LANES), F32),
            pltpu.VMEM((units, TILE, LANES), F32),
            pltpu.VMEM((units, TILE, LANES), F32),
            pltpu.VMEM((CHUNKS, swaps, kept, TILE, LANES), F32),
            pltpu.VMEM((CHUNKS, swaps, kept, TILE, LANES), F32),
            pltpu.VMEM((height, rank), F32),
            pltpu.VMEM((2 * rank, height), BF16),
            pltpu.VMEM((bits + 1, rank, rank), F32),
            pltpu.VMEM((bits, rank, rank), F32),
            pltpu.VMEM((rank, 2 * rank), F32),
            pltpu.VMEM((PANEL, rank), F32),
            pltpu.VMEM((height, 2 * rank), F32),
            pltpu.SemaphoreType.DMA((width // LOAD,)),
            pltpu.SemaphoreType.DMA,
            pltpu.SemaphoreType.DMA((CHUNKS, 2 * halves + swaps)),
            pltpu.SemaphoreType.DMA((CHUNKS, 2 * halves + swaps)),
            pltpu.SemaphoreType.DMA((bits,)),
            pltpu.SemaphoreType.DMA((bits,)),
            pltpu.SemaphoreType.DMA((CHUNKS,)),
            pltpu.SemaphoreType.DMA,
        ],
        compiler_params=pltpu.CompilerParams(
            collective_id=0, has_side_effects=True, vmem_limit_bytes=56 * 2**20
        ),
    )(slab, sketch)
    return pl.pallas_call(
        hand_over,
        out_shape=(
            jax.ShapeDtypeStruct((height, rank), F32),
            jax.ShapeDtypeStruct((rank, width), F32),
        ),
        in_specs=[anywhere] * 2,
        out_specs=(anywhere,) * 2,
        scratch_shapes=[
            pltpu.VMEM((height, rank), F32),
            pltpu.VMEM((rank // TILE, TILE, width), F32),
            pltpu.SemaphoreType.DMA((rank // TILE + 1,)),
            pltpu.SemaphoreType.DMA((rank // TILE + 1,)),
        ],
        compiler_params=pltpu.CompilerParams(vmem_limit_bytes=56 * 2**20),
    )(basis, projection)


def solution(mesh):
    rows, cols = mesh.shape["row"], mesh.shape["col"]
    placed = (P(("row", "col"), None), P())
    return jax.shard_map(
        functools.partial(per_device, rows, cols),
        mesh=mesh,
        in_specs=placed,
        out_specs=placed,
        check_vma=False,
    )
```
